32 devices in a mesh: row: 2 (over y), col: 16 (over z, x, core).
Axes of the slice: x: 2, y: 2, z: 4, core: 2. Of those that a mesh axis runs over, the one named last changes fastest.
Arguments:
- a_values: float32 [16, 16, 1, 5, 256, 256], P('row', 'col'), may hold values from -6 to 6
- a_columns: int32 [16, 16, 1, 5], P('row', 'col'), may hold values from 0 to 16, as said below
- b_values: float32 [16, 16, 1, 5, 256, 256], P('row', 'col'), may hold values from -0.375 to 0.375
- b_rows: int32 [16, 16, 1, 5], P('row', 'col'), may hold values from 0 to 16, as said below
Outputs:
- product: float32 [16, 16, 1, 1, 256, 256], P('row', 'col')
The draws below stay inside these ranges and needn't reach their ends.
Inputs may be any that keep to these rules, and one draw needn't show every extreme that they name: `a_columns`: in each row of slots the values below 16 are distinct and come first; 16 marks an empty slot; every row has at least one occupied slot. `b_rows`: in each row of slots the values below 16 are distinct and come first; 16 marks an empty slot; every row has at least one occupied slot.
All inputs are finite; a program needn't handle non-finite values.
Results may differ from the reference program's by a relative error of at most 0.0003.
Values sent between devices are 32-bit elements; how exact they have to be, the bound alone decides.
A program may use at most 256 MiB of HBM per device.

```python
import jax
import jax.numpy as jnp
from jax import lax

BS = 256
KB = 16
OCC = 5
RB = 1
CB = 1
SECTIONS = 4
GRID = 16


def slot_pattern(key, count_rows):
    first_key, second_key = jax.random.split(key)
    scores = jax.random.randint(first_key, (count_rows, KB), 0, 1 << 20) * KB + jnp.arange(KB, dtype=jnp.int32)[None, :]
    picks = jnp.argsort(scores, axis=-1)[:, :OCC].astype(jnp.int32)
    counts = jax.random.randint(second_key, (count_rows, 1), max(1, OCC - 2), OCC + 1)
    counts = counts.at[0, 0].set(OCC)
    counts = counts.at[1, 0].set(OCC - 1)
    slots = jnp.arange(OCC, dtype=jnp.int32)[None, :]
    return jnp.where(slots < counts, picks, KB).astype(jnp.int32)


def draw_a_columns(key, part):
    key = jax.random.fold_in(key, 11)
    return slot_pattern(key, GRID * GRID * RB).reshape(GRID, GRID, RB, OCC)


def draw_b_rows(key, part):
    key = jax.random.fold_in(key, 12)
    return slot_pattern(key, GRID * GRID * CB).reshape(GRID, GRID, CB, OCC)


def steps_of(key, dims, pieces, low, largest):
    gain, own = 1.0, jax.random.fold_in(key, 6)
    for position, shards_of in pieces:
        heights = jnp.exp(jax.random.uniform(jax.random.fold_in(own, position), (shards_of,), jnp.float32, low / len(pieces), largest / len(pieces)))
        gain = gain * jnp.repeat(heights, dims[position] // shards_of).reshape([-1 if axis == position else 1 for axis in range(len(dims))])
    return gain


def bell_draw(own_key, shape, spread, most, shards=(), kind=jnp.bfloat16):
    level = steps_of(own_key, shape, shards, -0.22, 0.18) if shards else 1.0
    entries = jax.random.normal(own_key, shape, jnp.float32) * spread * level
    return jnp.minimum(jnp.maximum(entries, -most), most).astype(kind)


def setup_inputs(seed: int = 0) -> dict:
    arg_keys = jax.random.split(jax.random.key(seed), 5)
    a_values = bell_draw(arg_keys[0], (GRID, GRID, RB, OCC, BS, BS), 1.0, 6.0, ((0, 2), (1, 16)), jnp.float32)
    a_columns = draw_a_columns(jax.random.fold_in(arg_keys[4], 71), 0)
    b_values = bell_draw(arg_keys[2], (GRID, GRID, CB, OCC, BS, BS), BS ** -0.5, 0.375, ((0, 2), (1, 16)), jnp.float32)
    b_rows = draw_b_rows(jax.random.fold_in(arg_keys[4], 71), 0)
    return {"a_values": a_values, "a_columns": a_columns, "b_values": b_values, "b_rows": b_rows}


def row_product(a_values, a_columns, b_values, b_rows, tile_row):
    running = jnp.zeros((GRID, RB, CB, BS, BS), jnp.float32)
    for section_num in range(SECTIONS):
        a_vals = jnp.roll(a_values[tile_row], -section_num, axis=0)
        a_cols = jnp.roll(a_columns[tile_row], -section_num, axis=0)
        source = ((tile_row + section_num) % GRID).astype(jnp.int32)
        b_vals = b_values[source]
        b_idx = b_rows[source]
        matches = ((a_cols[:, :, :, None, None] == b_idx[:, None, None, :, :])
                   & (a_cols < KB)[:, :, :, None, None]).astype(jnp.float32)
        chosen = jnp.einsum('jrocp,jcpxy->jrocxy', matches, b_vals, precision=lax.Precision.HIGHEST)
        running = running + jnp.einsum('jroxy,jrocyz->jrcxz', a_vals, chosen, precision=lax.Precision.HIGHEST)
    return running


def reference(a_values, a_columns, b_values, b_rows):
    return lax.map(lambda tile_row: row_product(a_values, a_columns, b_values, b_rows, tile_row),
                   jnp.arange(GRID, dtype=jnp.int32))
```

```python
import functools

import jax
import jax.numpy as jnp
from jax import lax
from jax.experimental import pallas as pl
from jax.experimental.pallas import tpu as pltpu
from jax.sharding import PartitionSpec as P

KB = 16
SECTIONS = 4
HALO = SECTIONS - 1
MESH = pl.DeviceIdType.MESH
LADDER = ((12, 10), (16, 12), (20, 15), (24, 20))
CHUNK = 4
BUFFERS = 8
LANES = 128
SEND_NEAR, SEND_ONE, PICK, RECV_NEAR, RECV_ONE, LEVEL = 0, 5, 10, 30, 40, 64


def ladder(slots):
    return tuple(step for step in LADDER if max(step) < slots) + ((slots, slots),)


def plan_kernel(rows, a_ref, b_ref, out_ref, grid_ref):
    occ, grid_rows, grid_cols = a_ref.shape
    me = lax.axis_index("col")
    core = lax.rem(me, 2)
    first = pl.multiple_of(lax.axis_index("row") * rows, rows)
    lane = lax.broadcasted_iota(jnp.int32, (grid_rows, grid_cols), 1)
    even = lax.rem(lane, 2) == 0
    small_lane = lax.broadcasted_iota(jnp.int32, (rows, grid_cols), 1)
    out_lane = lax.broadcasted_iota(jnp.int32, (rows, LANES), 1)
    result = jnp.zeros((rows, LANES), jnp.int32)

    def own(result, values, column, at):
        grid_ref[...] = values
        mine = grid_ref[pl.ds(first, rows), :]
        mine = jnp.sum(jnp.where(small_lane == column, mine, 0), axis=1, keepdims=True)
        return jnp.where(out_lane == at, mine, result)

    near_sum = jnp.zeros((grid_rows, grid_cols), jnp.int32)
    one_sum = jnp.zeros((grid_rows, grid_cols), jnp.int32)
    near_source = me - core + 2
    for o in range(occ):
        a = a_ref[o]
        picks = []
        for s in range(SECTIONS):
            pick = jnp.full((grid_rows, grid_cols), 0, jnp.int32)
            for p in range(occ):
                b = b_ref[p, s:s + grid_rows, HALO - s:HALO - s + grid_cols]
                pick = jnp.where((a == b) & (a < KB), p + 1, pick)
            picks.append(pick)
            result = own(result, pick, lax.rem(me + s, grid_cols), PICK + s * occ + o)
        used = [jnp.where(pick > 0, 1, 0) for pick in picks]
        near = jnp.where(even, jnp.maximum(used[1], used[2]), jnp.maximum(used[2], used[3]))
        one = jnp.where(even, used[3], used[1])
        near_sum += near
        one_sum += one
        result = own(result, near, me, SEND_NEAR + o)
        result = own(result, one, me, SEND_ONE + o)
        for k in range(2):
            result = own(result, near, lax.rem(near_source + k, grid_cols), RECV_NEAR + k * occ + o)
        result = own(result, one, lax.rem(me + 1 + 2 * core, grid_cols), RECV_ONE + o)
    level = jnp.zeros((1, 1), jnp.int32)
    near_most = jnp.zeros((1, grid_cols), jnp.int32)
    one_most = jnp.zeros((1, grid_cols), jnp.int32)
    for r in range(grid_rows // rows):
        part = slice(r * rows, (r + 1) * rows)
        near_most = jnp.maximum(near_most, jnp.sum(near_sum[part], axis=0, keepdims=True))
        one_most = jnp.maximum(one_most, jnp.sum(one_sum[part], axis=0, keepdims=True))
    near_most = jnp.max(near_most, axis=1, keepdims=True)
    one_most = jnp.max(one_most, axis=1, keepdims=True)
    for c2, c1 in ladder(rows * occ)[:-1]:
        level += jnp.where((near_most > c2) | (one_most > c1), 1, 0)
    out_ref[...] = jnp.where(out_lane == LEVEL, level, result)


def pack_kernel(occ, plan_ref, a_ref, near_ref, one_ref, sems):
    rows = plan_ref.shape[0]

    def each(act):
        def row(v, counts):
            near, one = counts
            for o in range(occ):
                take_near = plan_ref[v, SEND_NEAR + o]
                take_one = plan_ref[v, SEND_ONE + o]

                @pl.when(take_near > 0)
                def _(o=o, near=near):
                    act(pltpu.make_async_copy(a_ref.at[v * occ + o], near_ref.at[near], sems.at[0, near]))

                @pl.when(take_one > 0)
                def _(o=o, one=one):
                    act(pltpu.make_async_copy(a_ref.at[v * occ + o], one_ref.at[one], sems.at[1, one]))

                near, one = near + take_near, one + take_one
            return near, one

        lax.fori_loop(0, rows, row, (jnp.int32(0), jnp.int32(0)))

    each(lambda copy: copy.start())
    each(lambda copy: copy.wait())


def exchange_kernel(c2, c1, n, packed_near, packed_one, near_ref, one_ref,
                    near_send, near_recv, fwd_send, fwd_recv, one_send, one_recv):
    me = lax.axis_index("col")
    core = lax.rem(me, 2)
    near_to, near_from = lax.rem(me + n - 2, n), lax.rem(me + 2, n)
    one_to, one_from = lax.rem(me + n - 3 + 2 * core, n), lax.rem(me + 1 + 2 * core, n)
    sibling = me + 1 - 2 * core
    barrier = pltpu.get_barrier_semaphore()
    for other in (near_to, near_from, one_to, one_from):
        pl.semaphore_signal(barrier, inc=1, device_id={"col": other}, device_id_type=MESH)
    pl.semaphore_wait(barrier, 4)

    chunks = c2 // CHUNK
    near, forward = [], []
    for c in range(chunks):
        part = pl.ds(c * CHUNK, CHUNK)
        near.append(pltpu.make_async_remote_copy(
            src_ref=packed_near.at[part], dst_ref=near_ref.at[core, part],
            send_sem=near_send.at[c], recv_sem=near_recv.at[c],
            device_id={"col": near_to}, device_id_type=MESH))
        forward.append(pltpu.make_async_remote_copy(
            src_ref=near_ref.at[core, part], dst_ref=near_ref.at[core, part],
            send_sem=fwd_send.at[c], recv_sem=fwd_recv.at[c],
            device_id={"col": sibling}, device_id_type=MESH))
    one = pltpu.make_async_remote_copy(
        src_ref=packed_one.at[pl.ds(0, c1)], dst_ref=one_ref,
        send_sem=one_send, recv_sem=one_recv,
        device_id={"col": one_to}, device_id_type=MESH)
    near[0].start()
    one.start()
    for copy in near[1:]:
        copy.start()
    for c in range(chunks):
        near[c].wait_recv()
        forward[c].start()
    one.wait()
    for c in range(chunks):
        near[c].wait_send()
        forward[c].wait()


def product_kernel(occ, c2, plan_ref, a_ref, b_ref, halo_ref, near_ref, one_ref, out_ref,
                   a_items, b_items, v_items, a_buf, b_buf, a_sem, b_sem):
    rows = plan_ref.shape[0]
    odd = lax.rem(lax.axis_index("col"), 2)
    own = rows * occ
    near_end = own + 2 * c2

    def row(v, carry):
        count, near0, near1, one = carry
        for o in range(occ):
            at_near0 = own + near0
            at_near1 = own + c2 + near1
            at_one = near_end + one
            sources = (v * occ + o,
                       jnp.where(odd == 1, at_near0, at_one),
                       jnp.where(odd == 1, at_near1, at_near0),
                       jnp.where(odd == 1, at_one, at_near1))
            for s in range(SECTIONS):
                pick = plan_ref[v, PICK + s * occ + o]
                a_items[count] = sources[s]
                b_items[count] = (v + s) * occ + pick - 1
                v_items[count] = v
                count = count + jnp.where(pick > 0, 1, 0)
            near0 = near0 + plan_ref[v, RECV_NEAR + o]
            near1 = near1 + plan_ref[v, RECV_NEAR + occ + o]
            one = one + plan_ref[v, RECV_ONE + o]
        return count, near0, near1, one

    zero = jnp.int32(0)
    count, _, _, _ = lax.fori_loop(0, rows, row, (zero, zero, zero, zero))
    out_ref[...] = jnp.zeros_like(out_ref)

    def fetch(i):
        slot = lax.rem(i, BUFFERS)
        a_at, b_at = a_items[i], b_items[i]

        @pl.when(a_at < own)
        def _():
            pltpu.make_async_copy(a_ref.at[a_at], a_buf.at[slot], a_sem.at[slot]).start()

        @pl.when((a_at >= own) & (a_at < near_end))
        def _():
            pltpu.make_async_copy(near_ref.at[a_at - own], a_buf.at[slot], a_sem.at[slot]).start()

        @pl.when(a_at >= near_end)
        def _():
            pltpu.make_async_copy(one_ref.at[a_at - near_end], a_buf.at[slot], a_sem.at[slot]).start()

        @pl.when(b_at < own)
        def _():
            pltpu.make_async_copy(b_ref.at[b_at], b_buf.at[slot], b_sem.at[slot]).start()

        @pl.when(b_at >= own)
        def _():
            pltpu.make_async_copy(halo_ref.at[b_at - own], b_buf.at[slot], b_sem.at[slot]).start()

    def ahead(i, carry):
        fetch(i)
        return carry

    lax.fori_loop(0, jnp.minimum(count, BUFFERS - 1), ahead, 0)

    def item(i, carry):
        @pl.when(i + BUFFERS - 1 < count)
        def _():
            fetch(i + BUFFERS - 1)

        slot = lax.rem(i, BUFFERS)
        pltpu.make_async_copy(a_ref.at[0], a_buf.at[slot], a_sem.at[slot]).wait()
        pltpu.make_async_copy(b_ref.at[0], b_buf.at[slot], b_sem.at[slot]).wait()
        a, b = a_buf[slot], b_buf[slot]
        a_hi, b_hi = a.astype(jnp.bfloat16), b.astype(jnp.bfloat16)
        a_lo = (a - a_hi.astype(jnp.float32)).astype(jnp.bfloat16)
        b_lo = (b - b_hi.astype(jnp.float32)).astype(jnp.bfloat16)
        dot = functools.partial(jnp.dot, preferred_element_type=jnp.float32)
        v = v_items[i]
        out_ref[v] += dot(a_hi, b_hi) + (dot(a_hi, b_lo) + dot(a_lo, b_hi))
        return carry

    lax.fori_loop(0, count, item, 0)


def local(a_values, a_columns, b_values, b_rows):
    rows, _, _, occ, bs, _ = a_values.shape
    n_rows, n_cols = lax.axis_size("row"), lax.axis_size("col")
    block = (bs, bs)
    a_own = a_values.reshape(rows * occ, *block)
    b_own = b_values.reshape(rows * occ, *block)

    with jax.named_scope("b_halo"):
        route = [((i + 1) % n_rows, i) for i in range(n_rows)]
        halo = lax.ppermute(b_own[:HALO * occ], "row", route)

    with jax.named_scope("indices"):
        both = jnp.concatenate([a_columns[:, 0, 0], b_rows[:, 0, 0]], axis=1)
        gathered = lax.all_gather(both, ("row", "col"))
        gathered = gathered.reshape(n_rows, n_cols, rows, 2 * occ).transpose(3, 0, 2, 1)
        gathered = gathered.reshape(2 * occ, n_rows * rows, n_cols)
        a_grid, b_grid = gathered[:occ], gathered[occ:]
        b_grid = jnp.concatenate([b_grid, b_grid[:, :HALO]], axis=1)
        b_grid = jnp.concatenate([b_grid[:, :, -HALO:], b_grid], axis=2)

    vmem = pl.BlockSpec(memory_space=pltpu.VMEM)
    smem = pl.BlockSpec(memory_space=pltpu.SMEM)
    any_ = pl.BlockSpec(memory_space=pl.ANY)
    f32 = jnp.float32
    plan = pl.pallas_call(
        functools.partial(plan_kernel, rows),
        out_shape=jax.ShapeDtypeStruct((rows, LANES), jnp.int32),
        in_specs=[vmem, vmem],
        out_specs=vmem,
        scratch_shapes=[pltpu.VMEM((n_rows * rows, n_cols), jnp.int32)],
        name="plan",
    )(a_grid, b_grid)

    slots = rows * occ
    packed_near, packed_one = pl.pallas_call(
        functools.partial(pack_kernel, occ),
        out_shape=[jax.ShapeDtypeStruct((slots, *block), f32)] * 2,
        in_specs=[smem, any_],
        out_specs=[any_, any_],
        scratch_shapes=[pltpu.SemaphoreType.DMA((2, slots))],
        name="pack",
    )(plan, a_own)

    def branch(number, c2, c1):
        def run(plan, a_own, b_own, halo, packed_near, packed_one):
            dma = pltpu.SemaphoreType.DMA
            chunks = c2 // CHUNK
            near, one = pl.pallas_call(
                functools.partial(exchange_kernel, c2, c1, n_cols),
                out_shape=[jax.ShapeDtypeStruct((2, c2, *block), f32),
                           jax.ShapeDtypeStruct((c1, *block), f32)],
                in_specs=[any_, any_],
                out_specs=[any_, any_],
                scratch_shapes=[dma((chunks,)), dma((chunks,)), dma((chunks,)), dma((chunks,)), dma, dma],
                compiler_params=pltpu.CompilerParams(collective_id=number, has_side_effects=True),
                name="exchange",
            )(packed_near, packed_one)
            items = pltpu.SMEM((rows * occ * SECTIONS + 8,), jnp.int32)
            return pl.pallas_call(
                functools.partial(product_kernel, occ, c2),
                out_shape=jax.ShapeDtypeStruct((rows, *block), f32),
                in_specs=[smem] + [any_] * 5,
                out_specs=vmem,
                scratch_shapes=[items, items, items,
                                pltpu.VMEM((BUFFERS, *block), f32), pltpu.VMEM((BUFFERS, *block), f32),
                                dma((BUFFERS,)), dma((BUFFERS,))],
                compiler_params=pltpu.CompilerParams(vmem_limit_bytes=32 << 20),
                name="product",
            )(plan, a_own, b_own, halo, near.reshape(2 * c2, *block), one)

        return run

    branches = [branch(number, c2, c1) for number, (c2, c1) in enumerate(ladder(slots))]
    out = lax.switch(plan[0, LEVEL], branches, plan, a_own, b_own, halo, packed_near, packed_one)
    return out.reshape(rows, 1, 1, 1, *block)


def solution(mesh):
    return jax.shard_map(
        local,
        mesh=mesh,
        in_specs=(
            P("row", "col", None, None, None, None),
            P("row", "col", None, None),
            P("row", "col", None, None, None, None),
            P("row", "col", None, None),
        ),
        out_specs=P("row", "col", None, None, None, None),
        check_vma=False,
    )
```

```python
import functools

import jax
import jax.numpy as jnp
from jax import lax
from jax.experimental import pallas as pl
from jax.experimental.pallas import tpu as pltpu
from jax.sharding import PartitionSpec as P

KB = 16
SECTIONS = 4
HALO = SECTIONS - 1
MESH = pl.DeviceIdType.MESH
LADDER = ((12, 10), (16, 12), (20, 15), (24, 20))
CHUNK = 4
BUFFERS = 8
LANES = 128
SEND_NEAR, SEND_ONE, PICK, RECV_NEAR, RECV_ONE, LEVEL = 0, 5, 10, 30, 40, 64


def ladder(slots):
    return tuple(step for step in LADDER if max(step) < slots) + ((slots, slots),)


def plan_kernel(rows, a_ref, b_ref, out_ref, grid_ref):
    occ, grid_rows, grid_cols = a_ref.shape
    me = lax.axis_index("col")
    core = lax.rem(me, 2)
    first = pl.multiple_of(lax.axis_index("row") * rows, rows)
    lane = lax.broadcasted_iota(jnp.int32, (grid_rows, grid_cols), 1)
    even = lax.rem(lane, 2) == 0
    small_lane = lax.broadcasted_iota(jnp.int32, (rows, grid_cols), 1)
    out_lane = lax.broadcasted_iota(jnp.int32, (rows, LANES), 1)
    result = jnp.zeros((rows, LANES), jnp.int32)

    def own(result, values, column, at):
        grid_ref[...] = values
        mine = grid_ref[pl.ds(first, rows), :]
        mine = jnp.sum(jnp.where(small_lane == column, mine, 0), axis=1, keepdims=True)
        return jnp.where(out_lane == at, mine, result)

    near_sum = jnp.zeros((grid_rows, grid_cols), jnp.int32)
    one_sum = jnp.zeros((grid_rows, grid_cols), jnp.int32)
    near_source = me - core + 2
    for o in range(occ):
        a = a_ref[o]
        picks = []
        for s in range(SECTIONS):
            pick = jnp.full((grid_rows, grid_cols), 0, jnp.int32)
            for p in range(occ):
                b = b_ref[p, s:s + grid_rows, HALO - s:HALO - s + grid_cols]
                pick = jnp.where((a == b) & (a < KB), p + 1, pick)
            picks.append(pick)
            result = own(result, pick, lax.rem(me + s, grid_cols), PICK + s * occ + o)
        used = [jnp.where(pick > 0, 1, 0) for pick in picks]
        near = jnp.where(even, jnp.maximum(used[1], used[2]), jnp.maximum(used[2], used[3]))
        one = jnp.where(even, used[3], used[1])
        near_sum += near
        one_sum += one
        result = own(result, near, me, SEND_NEAR + o)
        result = own(result, one, me, SEND_ONE + o)
        for k in range(2):
            result = own(result, near, lax.rem(near_source + k, grid_cols), RECV_NEAR + k * occ + o)
        result = own(result, one, lax.rem(me + 1 + 2 * core, grid_cols), RECV_ONE + o)
    level = jnp.zeros((1, 1), jnp.int32)
    near_most = jnp.zeros((1, grid_cols), jnp.int32)
    one_most = jnp.zeros((1, grid_cols), jnp.int32)
    for r in range(grid_rows // rows):
        part = slice(r * rows, (r + 1) * rows)
        near_most = jnp.maximum(near_most, jnp.sum(near_sum[part], axis=0, keepdims=True))
        one_most = jnp.maximum(one_most, jnp.sum(one_sum[part], axis=0, keepdims=True))
    near_most = jnp.max(near_most, axis=1, keepdims=True)
    one_most = jnp.max(one_most, axis=1, keepdims=True)
    for c2, c1 in ladder(rows * occ)[:-1]:
        level += jnp.where((near_most > c2) | (one_most > c1), 1, 0)
    out_ref[...] = jnp.where(out_lane == LEVEL, level, result)


def index_kernel(n_rows, n_cols, mine_ref, out_ref, row_send, row_recv, col_send, col_recv):
    row, col = lax.axis_index("row"), lax.axis_index("col")
    barrier = pltpu.get_barrier_semaphore()
    for d in range(1, n_rows):
        pl.semaphore_signal(barrier, inc=1, device_id={"row": lax.rem(row + d, n_rows)}, device_id_type=MESH)
    for d in range(1, n_cols):
        pl.semaphore_signal(barrier, inc=1, device_id={"col": lax.rem(col + d, n_cols)}, device_id_type=MESH)
    pl.semaphore_wait(barrier, n_rows + n_cols - 2)
    out_ref[col, row] = mine_ref[...]
    copies = [
        pltpu.make_async_remote_copy(
            src_ref=mine_ref, dst_ref=out_ref.at[col, row],
            send_sem=row_send.at[d - 1], recv_sem=row_recv.at[d - 1],
            device_id={"row": lax.rem(row + d, n_rows)}, device_id_type=MESH)
        for d in range(1, n_rows)
    ]
    for copy in copies:
        copy.start()
    for copy in copies:
        copy.wait()
    copies = [
        pltpu.make_async_remote_copy(
            src_ref=out_ref.at[col], dst_ref=out_ref.at[col],
            send_sem=col_send.at[d - 1], recv_sem=col_recv.at[d - 1],
            device_id={"col": lax.rem(col + d, n_cols)}, device_id_type=MESH)
        for d in range(1, n_cols)
    ]
    for copy in copies:
        copy.start()
    for copy in copies:
        copy.wait()


def pack_kernel(occ, plan_ref, a_ref, near_ref, one_ref, stage, in_sems, out_sems):
    rows = plan_ref.shape[0]

    def each(act):
        def row(v, counts):
            near, one = counts
            for o in range(occ):
                take_near = plan_ref[v, SEND_NEAR + o]
                take_one = plan_ref[v, SEND_ONE + o]
                act(v * occ + o, near, one, take_near, take_one)
                near, one = near + take_near, one + take_one
            return near, one

        lax.fori_loop(0, rows, row, (jnp.int32(0), jnp.int32(0)))

    def load(i):
        return pltpu.make_async_copy(a_ref.at[i], stage.at[i], in_sems.at[i])

    def store_near(i, near):
        return pltpu.make_async_copy(stage.at[i], near_ref.at[near], out_sems.at[0, near])

    def store_one(i, one):
        return pltpu.make_async_copy(stage.at[i], one_ref.at[one], out_sems.at[1, one])

    def start_loads(i, near, one, take_near, take_one):
        @pl.when(take_near + take_one > 0)
        def _():
            load(i).start()

    def start_stores(i, near, one, take_near, take_one):
        @pl.when(take_near + take_one > 0)
        def _():
            load(i).wait()

        @pl.when(take_near > 0)
        def _():
            store_near(i, near).start()

        @pl.when(take_one > 0)
        def _():
            store_one(i, one).start()

    def wait_stores(i, near, one, take_near, take_one):
        @pl.when(take_near > 0)
        def _():
            store_near(i, near).wait()

        @pl.when(take_one > 0)
        def _():
            store_one(i, one).wait()

    each(start_loads)
    each(start_stores)
    each(wait_stores)


def exchange_kernel(c2, c1, n_rows, n, packed_near, packed_one, b_ref, near_ref, one_ref, halo_ref,
                    near_send, near_recv, fwd_send, fwd_recv, one_send, one_recv, halo_send, halo_recv):
    me, my_row = lax.axis_index("col"), lax.axis_index("row")
    row_to, row_from = lax.rem(my_row + n_rows - 1, n_rows), lax.rem(my_row + 1, n_rows)
    core = lax.rem(me, 2)
    near_to, near_from = lax.rem(me + n - 2, n), lax.rem(me + 2, n)
    one_to, one_from = lax.rem(me + n - 3 + 2 * core, n), lax.rem(me + 1 + 2 * core, n)
    sibling = me + 1 - 2 * core
    barrier = pltpu.get_barrier_semaphore()
    for other in (near_to, near_from, one_to, one_from):
        pl.semaphore_signal(barrier, inc=1, device_id={"col": other}, device_id_type=MESH)
    for other in (row_to, row_from):
        pl.semaphore_signal(barrier, inc=1, device_id={"row": other}, device_id_type=MESH)
    pl.semaphore_wait(barrier, 6)

    halo = pltpu.make_async_remote_copy(
        src_ref=b_ref.at[pl.ds(0, halo_ref.shape[0])], dst_ref=halo_ref,
        send_sem=halo_send, recv_sem=halo_recv,
        device_id={"row": row_to}, device_id_type=MESH)
    chunks = c2 // CHUNK
    near, forward = [], []
    for c in range(chunks):
        part = pl.ds(c * CHUNK, CHUNK)
        near.append(pltpu.make_async_remote_copy(
            src_ref=packed_near.at[part], dst_ref=near_ref.at[core, part],
            send_sem=near_send.at[c], recv_sem=near_recv.at[c],
            device_id={"col": near_to}, device_id_type=MESH))
        forward.append(pltpu.make_async_remote_copy(
            src_ref=near_ref.at[core, part], dst_ref=near_ref.at[core, part],
            send_sem=fwd_send.at[c], recv_sem=fwd_recv.at[c],
            device_id={"col": sibling}, device_id_type=MESH))
    one = pltpu.make_async_remote_copy(
        src_ref=packed_one.at[pl.ds(0, c1)], dst_ref=one_ref,
        send_sem=one_send, recv_sem=one_recv,
        device_id={"col": one_to}, device_id_type=MESH)
    near[0].start()
    one.start()
    halo.start()
    for copy in near[1:]:
        copy.start()
    for c in range(chunks):
        near[c].wait_recv()
        forward[c].start()
    one.wait()
    halo.wait()
    for c in range(chunks):
        near[c].wait_send()
        forward[c].wait()


def product_kernel(occ, c2, plan_ref, a_ref, b_ref, halo_ref, near_ref, one_ref, out_ref,
                   a_items, b_items, v_items, a_buf, b_buf, a_sem, b_sem):
    rows = plan_ref.shape[0]
    odd = lax.rem(lax.axis_index("col"), 2)
    own = rows * occ
    near_end = own + 2 * c2

    def row(v, carry):
        count, near0, near1, one = carry
        for o in range(occ):
            at_near0 = own + near0
            at_near1 = own + c2 + near1
            at_one = near_end + one
            sources = (v * occ + o,
                       jnp.where(odd == 1, at_near0, at_one),
                       jnp.where(odd == 1, at_near1, at_near0),
                       jnp.where(odd == 1, at_one, at_near1))
            for s in range(SECTIONS):
                pick = plan_ref[v, PICK + s * occ + o]
                a_items[count] = sources[s]
                b_items[count] = (v + s) * occ + pick - 1
                v_items[count] = v
                count = count + jnp.where(pick > 0, 1, 0)
            near0 = near0 + plan_ref[v, RECV_NEAR + o]
            near1 = near1 + plan_ref[v, RECV_NEAR + occ + o]
            one = one + plan_ref[v, RECV_ONE + o]
        return count, near0, near1, one

    zero = jnp.int32(0)
    count, _, _, _ = lax.fori_loop(0, rows, row, (zero, zero, zero, zero))
    out_ref[...] = jnp.zeros_like(out_ref)

    def fetch(i):
        slot = lax.rem(i, BUFFERS)
        a_at, b_at = a_items[i], b_items[i]

        @pl.when(a_at < own)
        def _():
            pltpu.make_async_copy(a_ref.at[a_at], a_buf.at[slot], a_sem.at[slot]).start()

        @pl.when((a_at >= own) & (a_at < near_end))
        def _():
            pltpu.make_async_copy(near_ref.at[a_at - own], a_buf.at[slot], a_sem.at[slot]).start()

        @pl.when(a_at >= near_end)
        def _():
            pltpu.make_async_copy(one_ref.at[a_at - near_end], a_buf.at[slot], a_sem.at[slot]).start()

        @pl.when(b_at < own)
        def _():
            pltpu.make_async_copy(b_ref.at[b_at], b_buf.at[slot], b_sem.at[slot]).start()

        @pl.when(b_at >= own)
        def _():
            pltpu.make_async_copy(halo_ref.at[b_at - own], b_buf.at[slot], b_sem.at[slot]).start()

    def ahead(i, carry):
        fetch(i)
        return carry

    lax.fori_loop(0, jnp.minimum(count, BUFFERS - 1), ahead, 0)

    def item(i, carry):
        @pl.when(i + BUFFERS - 1 < count)
        def _():
            fetch(i + BUFFERS - 1)

        slot = lax.rem(i, BUFFERS)
        pltpu.make_async_copy(a_ref.at[0], a_buf.at[slot], a_sem.at[slot]).wait()
        pltpu.make_async_copy(b_ref.at[0], b_buf.at[slot], b_sem.at[slot]).wait()
        a, b = a_buf[slot], b_buf[slot]
        a_hi, b_hi = a.astype(jnp.bfloat16), b.astype(jnp.bfloat16)
        a_lo = (a - a_hi.astype(jnp.float32)).astype(jnp.bfloat16)
        b_lo = (b - b_hi.astype(jnp.float32)).astype(jnp.bfloat16)
        dot = functools.partial(jnp.dot, preferred_element_type=jnp.float32)
        v = v_items[i]
        out_ref[v] += dot(a_hi, b_hi) + (dot(a_hi, b_lo) + dot(a_lo, b_hi))
        return carry

    lax.fori_loop(0, count, item, 0)


def local(a_values, a_columns, b_values, b_rows):
    rows, _, _, occ, bs, _ = a_values.shape
    n_rows, n_cols = lax.axis_size("row"), lax.axis_size("col")
    block = (bs, bs)
    a_own = a_values.reshape(rows * occ, *block)
    b_own = b_values.reshape(rows * occ, *block)

    vmem = pl.BlockSpec(memory_space=pltpu.VMEM)
    smem = pl.BlockSpec(memory_space=pltpu.SMEM)
    any_ = pl.BlockSpec(memory_space=pl.ANY)
    dma = pltpu.SemaphoreType.DMA
    f32 = jnp.float32
    slots = rows * occ
    steps = ladder(slots)

    with jax.named_scope("indices"):
        both = jnp.concatenate([a_columns[:, 0, 0], b_rows[:, 0, 0]], axis=1)
        both = jnp.pad(both, ((0, 0), (0, LANES - 2 * occ)))
        gathered = pl.pallas_call(
            functools.partial(index_kernel, n_rows, n_cols),
            out_shape=jax.ShapeDtypeStruct((n_cols, n_rows, rows, LANES), jnp.int32),
            in_specs=[vmem],
            out_specs=vmem,
            scratch_shapes=[dma((max(n_rows - 1, 1),))] * 2 + [dma((n_cols - 1,))] * 2,
            compiler_params=pltpu.CompilerParams(collective_id=len(steps), has_side_effects=True),
            name="indices",
        )(both)
        gathered = gathered[..., :2 * occ].transpose(3, 1, 2, 0)
        gathered = gathered.reshape(2 * occ, n_rows * rows, n_cols)
        a_grid, b_grid = gathered[:occ], gathered[occ:]
        b_grid = jnp.concatenate([b_grid, b_grid[:, :HALO]], axis=1)
        b_grid = jnp.concatenate([b_grid[:, :, -HALO:], b_grid], axis=2)

    plan = pl.pallas_call(
        functools.partial(plan_kernel, rows),
        out_shape=jax.ShapeDtypeStruct((rows, LANES), jnp.int32),
        in_specs=[vmem, vmem],
        out_specs=vmem,
        scratch_shapes=[pltpu.VMEM((n_rows * rows, n_cols), jnp.int32)],
        name="plan",
    )(a_grid, b_grid)

    packed_near, packed_one = pl.pallas_call(
        functools.partial(pack_kernel, occ),
        out_shape=[jax.ShapeDtypeStruct((slots, *block), f32)] * 2,
        in_specs=[smem, any_],
        out_specs=[any_, any_],
        scratch_shapes=[pltpu.VMEM((slots, *block), f32), dma((slots,)), dma((2, slots))],
        compiler_params=pltpu.CompilerParams(vmem_limit_bytes=56 << 20),
        name="pack",
    )(plan, a_own)

    def branch(number, c2, c1):
        def run(plan, a_own, b_own, packed_near, packed_one):
            chunks = c2 // CHUNK
            near, one, halo = pl.pallas_call(
                functools.partial(exchange_kernel, c2, c1, n_rows, n_cols),
                out_shape=[jax.ShapeDtypeStruct((2, c2, *block), f32),
                           jax.ShapeDtypeStruct((c1, *block), f32),
                           jax.ShapeDtypeStruct((HALO * occ, *block), f32)],
                in_specs=[any_] * 3,
                out_specs=[any_] * 3,
                scratch_shapes=[dma((chunks,)), dma((chunks,)), dma((chunks,)), dma((chunks,)), dma, dma, dma, dma],
                compiler_params=pltpu.CompilerParams(collective_id=number, has_side_effects=True),
                name="exchange",
            )(packed_near, packed_one, b_own)
            items = pltpu.SMEM((rows * occ * SECTIONS + 8,), jnp.int32)
            return pl.pallas_call(
                functools.partial(product_kernel, occ, c2),
                out_shape=jax.ShapeDtypeStruct((rows, *block), f32),
                in_specs=[smem] + [any_] * 5,
                out_specs=vmem,
                scratch_shapes=[items, items, items,
                                pltpu.VMEM((BUFFERS, *block), f32), pltpu.VMEM((BUFFERS, *block), f32),
                                dma((BUFFERS,)), dma((BUFFERS,))],
                compiler_params=pltpu.CompilerParams(vmem_limit_bytes=56 << 20),
                name="product",
            )(plan, a_own, b_own, halo, near.reshape(2 * c2, *block), one)

        return run

    branches = [branch(number, c2, c1) for number, (c2, c1) in enumerate(steps)]
    out = lax.switch(plan[0, LEVEL], branches, plan, a_own, b_own, packed_near, packed_one)
    return out.reshape(rows, 1, 1, 1, *block)


def solution(mesh):
    return jax.shard_map(
        local,
        mesh=mesh,
        in_specs=(
            P("row", "col", None, None, None, None),
            P("row", "col", None, None),
            P("row", "col", None, None, None, None),
            P("row", "col", None, None),
        ),
        out_specs=P("row", "col", None, None, None, None),
        check_vma=False,
    )
```

```python
import functools

import jax
import jax.numpy as jnp
from jax import lax
from jax.experimental import pallas as pl
from jax.experimental.pallas import tpu as pltpu
from jax.sharding import PartitionSpec as P

KB = 16
SECTIONS = 4
HALO = SECTIONS - 1
MESH = pl.DeviceIdType.MESH
LADDER = ((8, 8), (12, 10), (16, 14), (18, 16), (20, 16), (22, 18), (24, 20), (30, 26))
CHUNK = 2
LAG = 2
BUFFERS = 8
LANES = 128
SEND_NEAR, SEND_ONE, PICK, RECV_NEAR, RECV_ONE, LEVEL = 0, 5, 10, 30, 40, 64


def ladder(slots):
    return tuple(step for step in LADDER if max(step) < slots) + ((slots, slots),)


def plan_kernel(rows, a_ref, b_ref, out_ref, grid_ref):
    occ, grid_rows, grid_cols = a_ref.shape
    me = lax.axis_index("col")
    core = lax.rem(me, 2)
    first = pl.multiple_of(lax.axis_index("row") * rows, rows)
    lane = lax.broadcasted_iota(jnp.int32, (grid_rows, grid_cols), 1)
    even = lax.rem(lane, 2) == 0
    small_lane = lax.broadcasted_iota(jnp.int32, (rows, grid_cols), 1)
    out_lane = lax.broadcasted_iota(jnp.int32, (rows, LANES), 1)
    result = jnp.zeros((rows, LANES), jnp.int32)

    def own(result, values, column, at):
        grid_ref[...] = values
        mine = grid_ref[pl.ds(first, rows), :]
        mine = jnp.sum(jnp.where(small_lane == column, mine, 0), axis=1, keepdims=True)
        return jnp.where(out_lane == at, mine, result)

    near_sum = jnp.zeros((grid_rows, grid_cols), jnp.int32)
    one_sum = jnp.zeros((grid_rows, grid_cols), jnp.int32)
    near_source = me - core + 2
    for o in range(occ):
        a = a_ref[o]
        picks = []
        for s in range(SECTIONS):
            pick = jnp.full((grid_rows, grid_cols), 0, jnp.int32)
            for p in range(occ):
                b = b_ref[p, s:s + grid_rows, HALO - s:HALO - s + grid_cols]
                pick = jnp.where((a == b) & (a < KB), p + 1, pick)
            picks.append(pick)
            result = own(result, pick, lax.rem(me + s, grid_cols), PICK + s * occ + o)
        used = [jnp.where(pick > 0, 1, 0) for pick in picks]
        near = jnp.where(even, jnp.maximum(used[1], used[2]), jnp.maximum(used[2], used[3]))
        one = jnp.where(even, used[3], used[1])
        near_sum += near
        one_sum += one
        result = own(result, near, me, SEND_NEAR + o)
        result = own(result, one, me, SEND_ONE + o)
        for k in range(2):
            result = own(result, near, lax.rem(near_source + k, grid_cols), RECV_NEAR + k * occ + o)
        result = own(result, one, lax.rem(me + 1 + 2 * core, grid_cols), RECV_ONE + o)
    level = jnp.zeros((1, 1), jnp.int32)
    near_most = jnp.zeros((1, grid_cols), jnp.int32)
    one_most = jnp.zeros((1, grid_cols), jnp.int32)
    for r in range(grid_rows // rows):
        part = slice(r * rows, (r + 1) * rows)
        near_most = jnp.maximum(near_most, jnp.sum(near_sum[part], axis=0, keepdims=True))
        one_most = jnp.maximum(one_most, jnp.sum(one_sum[part], axis=0, keepdims=True))
    near_most = jnp.max(near_most, axis=1, keepdims=True)
    one_most = jnp.max(one_most, axis=1, keepdims=True)
    for c2, c1 in ladder(rows * occ)[:-1]:
        level += jnp.where((near_most > c2) | (one_most > c1), 1, 0)
    out_ref[...] = jnp.where(out_lane == LEVEL, level, result)


def index_kernel(n_rows, n_cols, mine_ref, out_ref, row_send, row_recv, col_send, col_recv):
    row, col = lax.axis_index("row"), lax.axis_index("col")
    barrier = pltpu.get_barrier_semaphore()
    for d in range(1, n_rows):
        pl.semaphore_signal(barrier, inc=1, device_id={"row": lax.rem(row + d, n_rows)}, device_id_type=MESH)
    for d in range(1, n_cols):
        pl.semaphore_signal(barrier, inc=1, device_id={"col": lax.rem(col + d, n_cols)}, device_id_type=MESH)
    pl.semaphore_wait(barrier, n_rows + n_cols - 2)
    out_ref[col, row] = mine_ref[...]
    copies = [
        pltpu.make_async_remote_copy(
            src_ref=mine_ref, dst_ref=out_ref.at[col, row],
            send_sem=row_send.at[d - 1], recv_sem=row_recv.at[d - 1],
            device_id={"row": lax.rem(row + d, n_rows)}, device_id_type=MESH)
        for d in range(1, n_rows)
    ]
    for copy in copies:
        copy.start()
    for copy in copies:
        copy.wait()
    copies = [
        pltpu.make_async_remote_copy(
            src_ref=out_ref.at[col], dst_ref=out_ref.at[col],
            send_sem=col_send.at[d - 1], recv_sem=col_recv.at[d - 1],
            device_id={"col": lax.rem(col + d, n_cols)}, device_id_type=MESH)
        for d in range(1, n_cols)
    ]
    for copy in copies:
        copy.start()
    for copy in copies:
        copy.wait()


def pack_kernel(occ, plan_ref, a_ref, near_ref, one_ref, stage, in_sems, out_sems):
    rows = plan_ref.shape[0]

    def each(act):
        def row(v, counts):
            near, one = counts
            for o in range(occ):
                take_near = plan_ref[v, SEND_NEAR + o]
                take_one = plan_ref[v, SEND_ONE + o]
                act(v * occ + o, near, one, take_near, take_one)
                near, one = near + take_near, one + take_one
            return near, one

        lax.fori_loop(0, rows, row, (jnp.int32(0), jnp.int32(0)))

    def load(i):
        return pltpu.make_async_copy(a_ref.at[i], stage.at[i], in_sems.at[i])

    def store_near(i, near):
        return pltpu.make_async_copy(stage.at[i], near_ref.at[near], out_sems.at[0, near])

    def store_one(i, one):
        return pltpu.make_async_copy(stage.at[i], one_ref.at[one], out_sems.at[1, one])

    def start_loads(i, near, one, take_near, take_one):
        @pl.when(take_near + take_one > 0)
        def _():
            load(i).start()

    def start_stores(i, near, one, take_near, take_one):
        @pl.when(take_near + take_one > 0)
        def _():
            load(i).wait()

        @pl.when(take_near > 0)
        def _():
            store_near(i, near).start()

        @pl.when(take_one > 0)
        def _():
            store_one(i, one).start()

    def wait_stores(i, near, one, take_near, take_one):
        @pl.when(take_near > 0)
        def _():
            store_near(i, near).wait()

        @pl.when(take_one > 0)
        def _():
            store_one(i, one).wait()

    each(start_loads)
    each(start_stores)
    each(wait_stores)


def exchange_kernel(c2, c1, n_rows, n, packed_near, packed_one, b_ref, near_ref, one_ref, halo_ref, held,
                    near_send, near_recv, held_send, held_recv, fwd_send, fwd_recv,
                    one_send, one_recv, halo_send, halo_recv):
    me, my_row = lax.axis_index("col"), lax.axis_index("row")
    core, side = lax.rem(me, 2), lax.rem(me // 2, 2)
    relays = core + side == 1

    def at(distance):
        return lax.rem(me + n + distance, n)

    row_to, row_from = lax.rem(my_row + n_rows - 1, n_rows), lax.rem(my_row + 1, n_rows)
    one_to, one_from = at(2 * core - 3), at(1 + 2 * core)
    sibling = me + 1 - 2 * core
    held_to = at(2 - 6 * core)
    passed_to = at(6 * core - 4)
    barrier = pltpu.get_barrier_semaphore()
    for other in (one_to, one_from, at(2 - 4 * side)):
        pl.semaphore_signal(barrier, inc=1, device_id={"col": other}, device_id_type=MESH)
    for other in (row_to, row_from):
        pl.semaphore_signal(barrier, inc=1, device_id={"row": other}, device_id_type=MESH)

    @pl.when(relays)
    def _():
        for other in (at(4), at(-4)):
            pl.semaphore_signal(barrier, inc=1, device_id={"col": other}, device_id_type=MESH)
        pl.semaphore_wait(barrier, 7)

    @pl.when(jnp.logical_not(relays))
    def _():
        pl.semaphore_wait(barrier, 5)

    halo = pltpu.make_async_remote_copy(
        src_ref=b_ref.at[pl.ds(0, halo_ref.shape[0])], dst_ref=halo_ref,
        send_sem=halo_send, recv_sem=halo_recv,
        device_id={"row": row_to}, device_id_type=MESH)
    one = pltpu.make_async_remote_copy(
        src_ref=packed_one.at[pl.ds(0, c1)], dst_ref=one_ref,
        send_sem=one_send, recv_sem=one_recv,
        device_id={"col": one_to}, device_id_type=MESH)
    chunks = c2 // CHUNK
    straight, first, second, forward = [], [], [], []
    for c in range(chunks):
        part = pl.ds(c * CHUNK, CHUNK)
        straight.append(pltpu.make_async_remote_copy(
            src_ref=packed_near.at[part], dst_ref=near_ref.at[core, part],
            send_sem=near_send.at[c], recv_sem=near_recv.at[c],
            device_id={"col": at(-2)}, device_id_type=MESH))
        first.append(pltpu.make_async_remote_copy(
            src_ref=packed_near.at[part], dst_ref=held.at[part],
            send_sem=near_send.at[c], recv_sem=held_recv.at[c],
            device_id={"col": held_to}, device_id_type=MESH))
        second.append(pltpu.make_async_remote_copy(
            src_ref=held.at[part], dst_ref=near_ref.at[core, part],
            send_sem=held_send.at[c], recv_sem=near_recv.at[c],
            device_id={"col": passed_to}, device_id_type=MESH))
        forward.append(pltpu.make_async_remote_copy(
            src_ref=near_ref.at[core, part], dst_ref=near_ref.at[core, part],
            send_sem=fwd_send.at[c], recv_sem=fwd_recv.at[c],
            device_id={"col": sibling}, device_id_type=MESH))

    @pl.when(side == 1)
    def _():
        for copy in straight:
            copy.start()

    @pl.when(side == 0)
    def _():
        for copy in first:
            copy.start()

    one.start()
    halo.start()
    for c in range(chunks + LAG):
        if c < chunks:
            @pl.when(relays)
            def _(c=c):
                first[c].wait_recv()
                second[c].start()

        if c >= LAG:
            straight[c - LAG].wait_recv()
            forward[c - LAG].start()
    one.wait()
    halo.wait()
    for c in range(chunks):
        straight[c].wait_send()
        forward[c].wait()

    @pl.when(relays)
    def _():
        for copy in second:
            copy.wait_send()


def product_kernel(occ, c2, plan_ref, a_ref, b_ref, halo_ref, near_ref, one_ref, out_ref,
                   a_items, b_items, v_items, a_buf, b_buf, a_sem, b_sem):
    rows = plan_ref.shape[0]
    odd = lax.rem(lax.axis_index("col"), 2)
    own = rows * occ
    near_end = own + 2 * c2

    def row(v, carry):
        count, near0, near1, one = carry
        for o in range(occ):
            at_near0 = own + near0
            at_near1 = own + c2 + near1
            at_one = near_end + one
            sources = (v * occ + o,
                       jnp.where(odd == 1, at_near0, at_one),
                       jnp.where(odd == 1, at_near1, at_near0),
                       jnp.where(odd == 1, at_one, at_near1))
            for s in range(SECTIONS):
                pick = plan_ref[v, PICK + s * occ + o]
                a_items[count] = sources[s]
                b_items[count] = (v + s) * occ + pick - 1
                v_items[count] = v
                count = count + jnp.where(pick > 0, 1, 0)
            near0 = near0 + plan_ref[v, RECV_NEAR + o]
            near1 = near1 + plan_ref[v, RECV_NEAR + occ + o]
            one = one + plan_ref[v, RECV_ONE + o]
        return count, near0, near1, one

    zero = jnp.int32(0)
    count, _, _, _ = lax.fori_loop(0, rows, row, (zero, zero, zero, zero))
    out_ref[...] = jnp.zeros_like(out_ref)

    def fetch(i):
        slot = lax.rem(i, BUFFERS)
        a_at, b_at = a_items[i], b_items[i]

        @pl.when(a_at < own)
        def _():
            pltpu.make_async_copy(a_ref.at[a_at], a_buf.at[slot], a_sem.at[slot]).start()

        @pl.when((a_at >= own) & (a_at < near_end))
        def _():
            pltpu.make_async_copy(near_ref.at[a_at - own], a_buf.at[slot], a_sem.at[slot]).start()

        @pl.when(a_at >= near_end)
        def _():
            pltpu.make_async_copy(one_ref.at[a_at - near_end], a_buf.at[slot], a_sem.at[slot]).start()

        @pl.when(b_at < own)
        def _():
            pltpu.make_async_copy(b_ref.at[b_at], b_buf.at[slot], b_sem.at[slot]).start()

        @pl.when(b_at >= own)
        def _():
            pltpu.make_async_copy(halo_ref.at[b_at - own], b_buf.at[slot], b_sem.at[slot]).start()

    def ahead(i, carry):
        fetch(i)
        return carry

    lax.fori_loop(0, jnp.minimum(count, BUFFERS - 1), ahead, 0)

    def item(i, carry):
        @pl.when(i + BUFFERS - 1 < count)
        def _():
            fetch(i + BUFFERS - 1)

        slot = lax.rem(i, BUFFERS)
        pltpu.make_async_copy(a_ref.at[0], a_buf.at[slot], a_sem.at[slot]).wait()
        pltpu.make_async_copy(b_ref.at[0], b_buf.at[slot], b_sem.at[slot]).wait()
        a, b = a_buf[slot], b_buf[slot]
        a_hi, b_hi = a.astype(jnp.bfloat16), b.astype(jnp.bfloat16)
        a_lo = (a - a_hi.astype(jnp.float32)).astype(jnp.bfloat16)
        b_lo = (b - b_hi.astype(jnp.float32)).astype(jnp.bfloat16)
        dot = functools.partial(jnp.dot, preferred_element_type=jnp.float32)
        v = v_items[i]
        out_ref[v] += dot(a_hi, b_hi) + (dot(a_hi, b_lo) + dot(a_lo, b_hi))
        return carry

    lax.fori_loop(0, count, item, 0)


def local(a_values, a_columns, b_values, b_rows):
    rows, _, _, occ, bs, _ = a_values.shape
    n_rows, n_cols = lax.axis_size("row"), lax.axis_size("col")
    block = (bs, bs)
    a_own = a_values.reshape(rows * occ, *block)
    b_own = b_values.reshape(rows * occ, *block)

    vmem = pl.BlockSpec(memory_space=pltpu.VMEM)
    smem = pl.BlockSpec(memory_space=pltpu.SMEM)
    any_ = pl.BlockSpec(memory_space=pl.ANY)
    dma = pltpu.SemaphoreType.DMA
    f32 = jnp.float32
    slots = rows * occ
    steps = ladder(slots)

    with jax.named_scope("indices"):
        both = jnp.concatenate([a_columns[:, 0, 0], b_rows[:, 0, 0]], axis=1)
        both = jnp.pad(both, ((0, 0), (0, LANES - 2 * occ)))
        gathered = pl.pallas_call(
            functools.partial(index_kernel, n_rows, n_cols),
            out_shape=jax.ShapeDtypeStruct((n_cols, n_rows, rows, LANES), jnp.int32),
            in_specs=[vmem],
            out_specs=vmem,
            scratch_shapes=[dma((max(n_rows - 1, 1),))] * 2 + [dma((n_cols - 1,))] * 2,
            compiler_params=pltpu.CompilerParams(collective_id=len(steps), has_side_effects=True),
            name="indices",
        )(both)
        gathered = gathered[..., :2 * occ].transpose(3, 1, 2, 0)
        gathered = gathered.reshape(2 * occ, n_rows * rows, n_cols)
        a_grid, b_grid = gathered[:occ], gathered[occ:]
        b_grid = jnp.concatenate([b_grid, b_grid[:, :HALO]], axis=1)
        b_grid = jnp.concatenate([b_grid[:, :, -HALO:], b_grid], axis=2)

    plan = pl.pallas_call(
        functools.partial(plan_kernel, rows),
        out_shape=jax.ShapeDtypeStruct((rows, LANES), jnp.int32),
        in_specs=[vmem, vmem],
        out_specs=vmem,
        scratch_shapes=[pltpu.VMEM((n_rows * rows, n_cols), jnp.int32)],
        name="plan",
    )(a_grid, b_grid)

    packed_near, packed_one = pl.pallas_call(
        functools.partial(pack_kernel, occ),
        out_shape=[jax.ShapeDtypeStruct((slots, *block), f32)] * 2,
        in_specs=[smem, any_],
        out_specs=[any_, any_],
        scratch_shapes=[pltpu.VMEM((slots, *block), f32), dma((slots,)), dma((2, slots))],
        compiler_params=pltpu.CompilerParams(vmem_limit_bytes=56 << 20),
        name="pack",
    )(plan, a_own)

    def branch(number, c2, c1):
        def run(plan, a_own, b_own, packed_near, packed_one):
            chunks = c2 // CHUNK
            near, one, halo = pl.pallas_call(
                functools.partial(exchange_kernel, c2, c1, n_rows, n_cols),
                out_shape=[jax.ShapeDtypeStruct((2, c2, *block), f32),
                           jax.ShapeDtypeStruct((c1, *block), f32),
                           jax.ShapeDtypeStruct((HALO * occ, *block), f32)],
                in_specs=[any_] * 3,
                out_specs=[any_] * 3,
                scratch_shapes=[pltpu.VMEM((c2, *block), f32)] + [dma((chunks,))] * 6 + [dma] * 4,
                compiler_params=pltpu.CompilerParams(
                    collective_id=number, has_side_effects=True, vmem_limit_bytes=56 << 20),
                name="exchange",
            )(packed_near, packed_one, b_own)
            items = pltpu.SMEM((rows * occ * SECTIONS + 8,), jnp.int32)
            return pl.pallas_call(
                functools.partial(product_kernel, occ, c2),
                out_shape=jax.ShapeDtypeStruct((rows, *block), f32),
                in_specs=[smem] + [any_] * 5,
                out_specs=vmem,
                scratch_shapes=[items, items, items,
                                pltpu.VMEM((BUFFERS, *block), f32), pltpu.VMEM((BUFFERS, *block), f32),
                                dma((BUFFERS,)), dma((BUFFERS,))],
                compiler_params=pltpu.CompilerParams(vmem_limit_bytes=56 << 20),
                name="product",
            )(plan, a_own, b_own, halo, near.reshape(2 * c2, *block), one)

        return run

    branches = [branch(number, c2, c1) for number, (c2, c1) in enumerate(steps)]
    out = lax.switch(plan[0, LEVEL], branches, plan, a_own, b_own, packed_near, packed_one)
    return out.reshape(rows, 1, 1, 1, *block)


def solution(mesh):
    return jax.shard_map(
        local,
        mesh=mesh,
        in_specs=(
            P("row", "col", None, None, None, None),
            P("row", "col", None, None),
            P("row", "col", None, None, None, None),
            P("row", "col", None, None),
        ),
        out_specs=P("row", "col", None, None, None, None),
        check_vma=False,
    )
```

```python
import functools

import jax
import jax.numpy as jnp
from jax import lax
from jax.experimental import pallas as pl
from jax.experimental.pallas import tpu as pltpu
from jax.sharding import PartitionSpec as P

KB = 16
SECTIONS = 4
HALO = SECTIONS - 1
MESH = pl.DeviceIdType.MESH
LADDER = ((8, 8), (12, 12), (14, 14), (16, 16), (17, 16), (18, 16), (19, 18), (20, 18), (24, 20), (30, 26))
EXCESS = 6
CHUNK = 2
LAG = 2
BUFFERS = 8
LANES = 128
SEND_NEAR, SEND_ONE, PICK, RECV_NEAR, RECV_ONE, LEVEL, SIBLING = 0, 5, 10, 30, 40, 64, 65


def ladder(slots):
    return tuple(step for step in LADDER if max(step) < slots) + ((slots, slots),)


def excess(slots, c2):
    return min(EXCESS, (slots - c2) // CHUNK * CHUNK)


def plan_kernel(rows, a_ref, b_ref, out_ref, grid_ref):
    occ, grid_rows, grid_cols = a_ref.shape
    me = lax.axis_index("col")
    core = lax.rem(me, 2)
    first = pl.multiple_of(lax.axis_index("row") * rows, rows)
    lane = lax.broadcasted_iota(jnp.int32, (grid_rows, grid_cols), 1)
    even = lax.rem(lane, 2) == 0
    small_lane = lax.broadcasted_iota(jnp.int32, (rows, grid_cols), 1)
    out_lane = lax.broadcasted_iota(jnp.int32, (rows, LANES), 1)
    result = jnp.zeros((rows, LANES), jnp.int32)

    def own(result, values, column, at):
        grid_ref[...] = values
        mine = grid_ref[pl.ds(first, rows), :]
        mine = jnp.sum(jnp.where(small_lane == column, mine, 0), axis=1, keepdims=True)
        return jnp.where(out_lane == at, mine, result)

    near_sum = jnp.zeros((grid_rows, grid_cols), jnp.int32)
    one_sum = jnp.zeros((grid_rows, grid_cols), jnp.int32)
    near_source = me - core + 2
    for o in range(occ):
        a = a_ref[o]
        picks = []
        for s in range(SECTIONS):
            pick = jnp.full((grid_rows, grid_cols), 0, jnp.int32)
            for p in range(occ):
                b = b_ref[p, s:s + grid_rows, HALO - s:HALO - s + grid_cols]
                pick = jnp.where((a == b) & (a < KB), p + 1, pick)
            picks.append(pick)
            result = own(result, pick, lax.rem(me + s, grid_cols), PICK + s * occ + o)
        used = [jnp.where(pick > 0, 1, 0) for pick in picks]
        near = jnp.where(even, jnp.maximum(used[1], used[2]), jnp.maximum(used[2], used[3]))
        one = jnp.where(even, used[3], used[1])
        near_sum += near
        one_sum += one
        result = own(result, near, me, SEND_NEAR + o)
        result = own(result, one, me, SEND_ONE + o)
        for k in range(2):
            result = own(result, near, lax.rem(near_source + k, grid_cols), RECV_NEAR + k * occ + o)
        result = own(result, one, lax.rem(me + 1 + 2 * core, grid_cols), RECV_ONE + o)
    level = jnp.zeros((1, 1), jnp.int32)
    near_most = jnp.zeros((1, grid_cols), jnp.int32)
    pair_most = jnp.zeros((1, grid_cols), jnp.int32)
    one_most = jnp.zeros((1, grid_cols), jnp.int32)
    for r in range(grid_rows // rows):
        part = slice(r * rows, (r + 1) * rows)
        count = jnp.sum(near_sum[part], axis=0, keepdims=True)
        pair = jnp.where(even[:1], count + jnp.concatenate([count[:, 1:], count[:, :1]], axis=1), 0)
        pair_most = jnp.maximum(pair_most, pair)
        near_most = jnp.maximum(near_most, count)
        one_most = jnp.maximum(one_most, jnp.sum(one_sum[part], axis=0, keepdims=True))
    pair_most = jnp.max(pair_most, axis=1, keepdims=True)
    near_most = jnp.max(near_most, axis=1, keepdims=True)
    one_most = jnp.max(one_most, axis=1, keepdims=True)
    for c2, c1 in ladder(rows * occ)[:-1]:
        over = (pair_most > 2 * c2) | (near_most > c2 + excess(rows * occ, c2)) | (one_most > c1)
        level = jnp.maximum(level, jnp.where(over, 1 + ladder(rows * occ).index((c2, c1)), 0))
    grid_ref[...] = near_sum
    sibling = jnp.where(small_lane == me + 1 - 2 * core, grid_ref[pl.ds(first, rows), :], 0)
    sibling = jnp.sum(jnp.sum(sibling, axis=1, keepdims=True), axis=0, keepdims=True)
    result = jnp.where(out_lane == SIBLING, sibling, result)
    out_ref[...] = jnp.where(out_lane == LEVEL, level, result)


def index_kernel(n_rows, n_cols, mine_ref, out_ref, row_send, row_recv, col_send, col_recv):
    row, col = lax.axis_index("row"), lax.axis_index("col")
    barrier = pltpu.get_barrier_semaphore()
    for d in range(1, n_rows):
        pl.semaphore_signal(barrier, inc=1, device_id={"row": lax.rem(row + d, n_rows)}, device_id_type=MESH)
    for d in range(1, n_cols):
        pl.semaphore_signal(barrier, inc=1, device_id={"col": lax.rem(col + d, n_cols)}, device_id_type=MESH)
    pl.semaphore_wait(barrier, n_rows + n_cols - 2)
    out_ref[col, row] = mine_ref[...]
    copies = [
        pltpu.make_async_remote_copy(
            src_ref=mine_ref, dst_ref=out_ref.at[col, row],
            send_sem=row_send.at[d - 1], recv_sem=row_recv.at[d - 1],
            device_id={"row": lax.rem(row + d, n_rows)}, device_id_type=MESH)
        for d in range(1, n_rows)
    ]
    for copy in copies:
        copy.start()
    for copy in copies:
        copy.wait()
    copies = [
        pltpu.make_async_remote_copy(
            src_ref=out_ref.at[col], dst_ref=out_ref.at[col],
            send_sem=col_send.at[d - 1], recv_sem=col_recv.at[d - 1],
            device_id={"col": lax.rem(col + d, n_cols)}, device_id_type=MESH)
        for d in range(1, n_cols)
    ]
    for copy in copies:
        copy.start()
    for copy in copies:
        copy.wait()


def pack_kernel(occ, plan_ref, a_ref, near_ref, one_ref, stage, in_sems, out_sems):
    rows = plan_ref.shape[0]

    def each(act):
        def row(v, counts):
            near, one = counts
            for o in range(occ):
                take_near = plan_ref[v, SEND_NEAR + o]
                take_one = plan_ref[v, SEND_ONE + o]
                act(v * occ + o, near, one, take_near, take_one)
                near, one = near + take_near, one + take_one
            return near, one

        lax.fori_loop(0, rows, row, (jnp.int32(0), jnp.int32(0)))

    def load(i):
        return pltpu.make_async_copy(a_ref.at[i], stage.at[i], in_sems.at[i])

    def store_near(i, near):
        return pltpu.make_async_copy(stage.at[i], near_ref.at[near], out_sems.at[0, near])

    def store_one(i, one):
        return pltpu.make_async_copy(stage.at[i], one_ref.at[one], out_sems.at[1, one])

    def start_loads(i, near, one, take_near, take_one):
        @pl.when(take_near + take_one > 0)
        def _():
            load(i).start()

    def start_stores(i, near, one, take_near, take_one):
        @pl.when(take_near + take_one > 0)
        def _():
            load(i).wait()

        @pl.when(take_near > 0)
        def _():
            store_near(i, near).start()

        @pl.when(take_one > 0)
        def _():
            store_one(i, one).start()

    def wait_stores(i, near, one, take_near, take_one):
        @pl.when(take_near > 0)
        def _():
            store_near(i, near).wait()

        @pl.when(take_one > 0)
        def _():
            store_one(i, one).wait()

    each(start_loads)
    each(start_stores)
    each(wait_stores)


def parts_of(c2, spare):
    parts = []
    for low, high in ((0, c2 - spare), (c2 - spare, c2)):
        parts += [(start, min(CHUNK, high - start)) for start in range(low, high, CHUNK)]
    return parts


def exchange_kernel(c2, c1, spare, n_rows, n, plan_ref, packed_near, packed_one, b_ref,
                    near_ref, one_ref, halo_ref, held, tail, extra, tail_sem, extra_send, extra_recv,
                    near_send, near_recv, held_send, held_recv, fwd_send, fwd_recv,
                    one_send, one_recv, halo_send, halo_recv):
    me, my_row = lax.axis_index("col"), lax.axis_index("row")
    core, side = lax.rem(me, 2), lax.rem(me // 2, 2)
    relays = core + side == 1

    def at(distance):
        return lax.rem(me + n + distance, n)

    row_to, row_from = lax.rem(my_row + n_rows - 1, n_rows), lax.rem(my_row + 1, n_rows)
    one_to, one_from = at(2 * core - 3), at(1 + 2 * core)
    sibling = me + 1 - 2 * core
    held_to = at(2 - 6 * core)
    passed_to = at(6 * core - 4)
    barrier = pltpu.get_barrier_semaphore()
    for other in (one_to, one_from, at(2 - 4 * side)):
        pl.semaphore_signal(barrier, inc=1, device_id={"col": other}, device_id_type=MESH)
    for other in (row_to, row_from):
        pl.semaphore_signal(barrier, inc=1, device_id={"row": other}, device_id_type=MESH)

    @pl.when(relays)
    def _():
        for other in (at(4), at(-4)):
            pl.semaphore_signal(barrier, inc=1, device_id={"col": other}, device_id_type=MESH)
        pl.semaphore_wait(barrier, 7)

    @pl.when(jnp.logical_not(relays))
    def _():
        pl.semaphore_wait(barrier, 5)

    halo = pltpu.make_async_remote_copy(
        src_ref=b_ref.at[pl.ds(0, halo_ref.shape[0])], dst_ref=halo_ref,
        send_sem=halo_send, recv_sem=halo_recv,
        device_id={"row": row_to}, device_id_type=MESH)
    one = pltpu.make_async_remote_copy(
        src_ref=packed_one.at[pl.ds(0, c1)], dst_ref=one_ref,
        send_sem=one_send, recv_sem=one_recv,
        device_id={"col": one_to}, device_id_type=MESH)
    if spare:
        own_tail = pltpu.make_async_copy(packed_near.at[pl.ds(c2 - spare, spare)], tail, tail_sem)
        over = pltpu.make_async_remote_copy(
            src_ref=packed_near.at[pl.ds(c2, spare)], dst_ref=extra,
            send_sem=extra_send, recv_sem=extra_recv,
            device_id={"col": sibling}, device_id_type=MESH)
        over.start()
        own_tail.start()
    parts = parts_of(c2, spare)
    chunks = len(parts)
    straight, first, second, forward = [], [], [], []
    for c, (start, size) in enumerate(parts):
        part = pl.ds(start, size)
        if start >= c2 - spare:
            source = tail.at[pl.ds(start - (c2 - spare), size)]
        else:
            source = packed_near.at[part]
        straight.append(pltpu.make_async_remote_copy(
            src_ref=source, dst_ref=near_ref.at[core, part],
            send_sem=near_send.at[c], recv_sem=near_recv.at[c],
            device_id={"col": at(-2)}, device_id_type=MESH))
        first.append(pltpu.make_async_remote_copy(
            src_ref=source, dst_ref=held.at[part],
            send_sem=near_send.at[c], recv_sem=held_recv.at[c],
            device_id={"col": held_to}, device_id_type=MESH))
        second.append(pltpu.make_async_remote_copy(
            src_ref=held.at[part], dst_ref=near_ref.at[core, part],
            send_sem=held_send.at[c], recv_sem=near_recv.at[c],
            device_id={"col": passed_to}, device_id_type=MESH))
        forward.append(pltpu.make_async_remote_copy(
            src_ref=near_ref.at[core, part], dst_ref=near_ref.at[core, part],
            send_sem=fwd_send.at[c], recv_sem=fwd_recv.at[c],
            device_id={"col": sibling}, device_id_type=MESH))

    def send(some):
        @pl.when(side == 1)
        def _():
            for c in some:
                straight[c].start()

        @pl.when(side == 0)
        def _():
            for c in some:
                first[c].start()

    whole = [c for c in range(chunks) if parts[c][0] < c2 - spare]
    send(whole)
    one.start()
    halo.start()
    if spare:
        own_tail.wait()
        over.wait_recv()
        count = plan_ref[0:1, SIBLING:SIBLING + 1] - c2
        for t in range(spare):
            tail[spare - 1 - t] = jnp.where(count > t, extra[t], tail[spare - 1 - t])
        send(range(len(whole), chunks))
    for c in range(chunks + LAG):
        if c < chunks:
            @pl.when(relays)
            def _(c=c):
                first[c].wait_recv()
                second[c].start()

        if c >= LAG:
            straight[c - LAG].wait_recv()
            forward[c - LAG].start()
    one.wait()
    halo.wait()
    if spare:
        over.wait_send()
    for c in range(chunks):
        straight[c].wait_send()
        forward[c].wait()

    @pl.when(relays)
    def _():
        for copy in second:
            copy.wait_send()


def product_kernel(occ, c2, plan_ref, a_ref, b_ref, halo_ref, near_ref, one_ref, out_ref,
                   a_items, b_items, v_items, a_buf, b_buf, total, a_sem, b_sem, out_sem):
    rows = plan_ref.shape[0]
    odd = lax.rem(lax.axis_index("col"), 2)
    own = rows * occ
    near_end = own + 2 * c2

    def row(v, carry):
        count, near0, near1, one = carry
        for o in range(occ):
            at_near0 = own + jnp.where(near0 < c2, near0, 3 * c2 - 1 - near0)
            at_near1 = own + jnp.where(near1 < c2, c2 + near1, 2 * c2 - 1 - near1)
            at_one = near_end + one
            sources = (v * occ + o,
                       jnp.where(odd == 1, at_near0, at_one),
                       jnp.where(odd == 1, at_near1, at_near0),
                       jnp.where(odd == 1, at_one, at_near1))
            for s in range(SECTIONS):
                pick = plan_ref[v, PICK + s * occ + o]
                a_items[count] = sources[s]
                b_items[count] = (v + s) * occ + pick - 1
                v_items[count] = v
                count = count + jnp.where(pick > 0, 1, 0)
            near0 = near0 + plan_ref[v, RECV_NEAR + o]
            near1 = near1 + plan_ref[v, RECV_NEAR + occ + o]
            one = one + plan_ref[v, RECV_ONE + o]
        return count, near0, near1, one

    zero = jnp.int32(0)
    count, _, _, _ = lax.fori_loop(0, rows, row, (zero, zero, zero, zero))
    a_items[count] = 0
    b_items[count] = 0
    v_items[count] = rows
    count = (count + 1) // 2 * 2

    def fetch(i):
        slot = lax.rem(i, BUFFERS)
        a_at, b_at = a_items[i], b_items[i]

        @pl.when(a_at < own)
        def _():
            pltpu.make_async_copy(a_ref.at[a_at], a_buf.at[slot], a_sem.at[slot]).start()

        @pl.when((a_at >= own) & (a_at < near_end))
        def _():
            pltpu.make_async_copy(near_ref.at[a_at - own], a_buf.at[slot], a_sem.at[slot]).start()

        @pl.when(a_at >= near_end)
        def _():
            pltpu.make_async_copy(one_ref.at[a_at - near_end], a_buf.at[slot], a_sem.at[slot]).start()

        @pl.when(b_at < own)
        def _():
            pltpu.make_async_copy(b_ref.at[b_at], b_buf.at[slot], b_sem.at[slot]).start()

        @pl.when(b_at >= own)
        def _():
            pltpu.make_async_copy(halo_ref.at[b_at - own], b_buf.at[slot], b_sem.at[slot]).start()

    def ahead(i, carry):
        fetch(i)
        return carry

    lax.fori_loop(0, jnp.minimum(count, BUFFERS - 2), ahead, 0)
    total[...] = jnp.zeros_like(total)

    def multiply(slot):
        a, b = a_buf[slot], b_buf[slot]
        a_hi, b_hi = a.astype(jnp.bfloat16), b.astype(jnp.bfloat16)
        a_lo = (a - a_hi.astype(jnp.float32)).astype(jnp.bfloat16)
        b_lo = (b - b_hi.astype(jnp.float32)).astype(jnp.bfloat16)
        dot = functools.partial(jnp.dot, preferred_element_type=jnp.float32)
        return dot(a_hi, b_hi) + (dot(a_hi, b_lo) + dot(a_lo, b_hi))

    def pair(k, carry):
        i = 2 * k

        @pl.when(i + BUFFERS - 2 < count)
        def _():
            fetch(i + BUFFERS - 2)
            fetch(i + BUFFERS - 1)

        slots = lax.rem(i, BUFFERS), lax.rem(i + 1, BUFFERS)
        for slot in slots:
            pltpu.make_async_copy(a_ref.at[0], a_buf.at[slot], a_sem.at[slot]).wait()
            pltpu.make_async_copy(b_ref.at[0], b_buf.at[slot], b_sem.at[slot]).wait()
        left, right = multiply(slots[0]), multiply(slots[1])
        total[v_items[i]] += left
        total[v_items[i + 1]] += right
        return carry

    lax.fori_loop(0, count // 2, pair, 0)
    result = pltpu.make_async_copy(total.at[pl.ds(0, rows)], out_ref, out_sem)
    result.start()
    result.wait()


def local(a_values, a_columns, b_values, b_rows):
    rows, _, _, occ, bs, _ = a_values.shape
    n_rows, n_cols = lax.axis_size("row"), lax.axis_size("col")
    block = (bs, bs)
    a_own = a_values.reshape(rows * occ, *block)
    b_own = b_values.reshape(rows * occ, *block)

    vmem = pl.BlockSpec(memory_space=pltpu.VMEM)
    smem = pl.BlockSpec(memory_space=pltpu.SMEM)
    any_ = pl.BlockSpec(memory_space=pl.ANY)
    dma = pltpu.SemaphoreType.DMA
    f32 = jnp.float32
    slots = rows * occ
    steps = ladder(slots)

    with jax.named_scope("indices"):
        both = jnp.concatenate([a_columns[:, 0, 0], b_rows[:, 0, 0]], axis=1)
        both = jnp.pad(both, ((0, 0), (0, LANES - 2 * occ)))
        gathered = pl.pallas_call(
            functools.partial(index_kernel, n_rows, n_cols),
            out_shape=jax.ShapeDtypeStruct((n_cols, n_rows, rows, LANES), jnp.int32),
            in_specs=[vmem],
            out_specs=vmem,
            scratch_shapes=[dma((max(n_rows - 1, 1),))] * 2 + [dma((n_cols - 1,))] * 2,
            compiler_params=pltpu.CompilerParams(collective_id=len(steps), has_side_effects=True),
            name="indices",
        )(both)
        gathered = gathered[..., :2 * occ].transpose(3, 1, 2, 0)
        gathered = gathered.reshape(2 * occ, n_rows * rows, n_cols)
        a_grid, b_grid = gathered[:occ], gathered[occ:]
        b_grid = jnp.concatenate([b_grid, b_grid[:, :HALO]], axis=1)
        b_grid = jnp.concatenate([b_grid[:, :, -HALO:], b_grid], axis=2)

    plan = pl.pallas_call(
        functools.partial(plan_kernel, rows),
        out_shape=jax.ShapeDtypeStruct((rows, LANES), jnp.int32),
        in_specs=[vmem, vmem],
        out_specs=vmem,
        scratch_shapes=[pltpu.VMEM((n_rows * rows, n_cols), jnp.int32)],
        name="plan",
    )(a_grid, b_grid)

    packed_near, packed_one = pl.pallas_call(
        functools.partial(pack_kernel, occ),
        out_shape=[jax.ShapeDtypeStruct((slots, *block), f32)] * 2,
        in_specs=[smem, any_],
        out_specs=[any_, any_],
        scratch_shapes=[pltpu.VMEM((slots, *block), f32), dma((slots,)), dma((2, slots))],
        compiler_params=pltpu.CompilerParams(vmem_limit_bytes=56 << 20),
        name="pack",
    )(plan, a_own)

    def branch(number, c2, c1):
        def run(plan, a_own, b_own, packed_near, packed_one):
            spare = excess(slots, c2)
            chunks = len(parts_of(c2, spare))
            near, one, halo = pl.pallas_call(
                functools.partial(exchange_kernel, c2, c1, spare, n_rows, n_cols),
                out_shape=[jax.ShapeDtypeStruct((2, c2, *block), f32),
                           jax.ShapeDtypeStruct((c1, *block), f32),
                           jax.ShapeDtypeStruct((HALO * occ, *block), f32)],
                in_specs=[vmem] + [any_] * 3,
                out_specs=[any_] * 3,
                scratch_shapes=[pltpu.VMEM((c2, *block), f32)] + [pltpu.VMEM((max(spare, 1), *block), f32)] * 2
                + [dma] * 3 + [dma((chunks,))] * 6 + [dma] * 4,
                compiler_params=pltpu.CompilerParams(
                    collective_id=number, has_side_effects=True, vmem_limit_bytes=56 << 20),
                name="exchange",
            )(plan, packed_near, packed_one, b_own)
            items = pltpu.SMEM((rows * occ * SECTIONS + 8,), jnp.int32)
            return pl.pallas_call(
                functools.partial(product_kernel, occ, c2),
                out_shape=jax.ShapeDtypeStruct((rows, *block), f32),
                in_specs=[smem] + [any_] * 5,
                out_specs=any_,
                scratch_shapes=[items, items, items,
                                pltpu.VMEM((BUFFERS, *block), f32), pltpu.VMEM((BUFFERS, *block), f32),
                                pltpu.VMEM((rows + 1, *block), f32),
                                dma((BUFFERS,)), dma((BUFFERS,)), dma],
                compiler_params=pltpu.CompilerParams(vmem_limit_bytes=56 << 20),
                name="product",
            )(plan, a_own, b_own, halo, near.reshape(2 * c2, *block), one)

        return run

    branches = [branch(number, c2, c1) for number, (c2, c1) in enumerate(steps)]
    out = lax.switch(plan[0, LEVEL], branches, plan, a_own, b_own, packed_near, packed_one)
    return out.reshape(rows, 1, 1, 1, *block)


def solution(mesh):
    return jax.shard_map(
        local,
        mesh=mesh,
        in_specs=(
            P("row", "col", None, None, None, None),
            P("row", "col", None, None),
            P("row", "col", None, None, None, None),
            P("row", "col", None, None),
        ),
        out_specs=P("row", "col", None, None, None, None),
        check_vma=False,
    )
```

```python
import functools

import jax
import jax.numpy as jnp
from jax import lax
from jax.experimental import pallas as pl
from jax.experimental.pallas import tpu as pltpu
from jax.sharding import PartitionSpec as P

KB = 16
SECTIONS = 4
HALO = SECTIONS - 1
MESH = pl.DeviceIdType.MESH
LADDER = ((8, 8), (12, 12), (14, 14), (16, 16), (17, 16), (18, 16), (19, 18), (20, 18), (24, 20), (30, 26))
EXCESS = 6
CHUNK = 2
LAG = 4
BUFFERS = 8
LANES = 128
SEND_NEAR, SEND_ONE, PICK, RECV_NEAR, RECV_ONE, LEVEL, SIBLING = 0, 5, 10, 30, 40, 64, 65


def ladder(slots):
    return tuple(step for step in LADDER if max(step) < slots) + ((slots, slots),)


def excess(slots, c2):
    return min(EXCESS, (slots - c2) // CHUNK * CHUNK)


def plan_kernel(rows, a_ref, b_ref, out_ref, grid_ref):
    occ, grid_rows, grid_cols = a_ref.shape
    me = lax.axis_index("col")
    core = lax.rem(me, 2)
    first = pl.multiple_of(lax.axis_index("row") * rows, rows)
    lane = lax.broadcasted_iota(jnp.int32, (grid_rows, grid_cols), 1)
    even = lax.rem(lane, 2) == 0
    small_lane = lax.broadcasted_iota(jnp.int32, (rows, grid_cols), 1)
    out_lane = lax.broadcasted_iota(jnp.int32, (rows, LANES), 1)
    result = jnp.zeros((rows, LANES), jnp.int32)

    def own(result, values, column, at):
        grid_ref[...] = values
        mine = grid_ref[pl.ds(first, rows), :]
        mine = jnp.sum(jnp.where(small_lane == column, mine, 0), axis=1, keepdims=True)
        return jnp.where(out_lane == at, mine, result)

    near_sum = jnp.zeros((grid_rows, grid_cols), jnp.int32)
    one_sum = jnp.zeros((grid_rows, grid_cols), jnp.int32)
    near_source = me - core + 2
    for o in range(occ):
        a = a_ref[o]
        picks = []
        for s in range(SECTIONS):
            pick = jnp.full((grid_rows, grid_cols), 0, jnp.int32)
            for p in range(occ):
                b = b_ref[p, s:s + grid_rows, HALO - s:HALO - s + grid_cols]
                pick = jnp.where((a == b) & (a < KB), p + 1, pick)
            picks.append(pick)
            result = own(result, pick, lax.rem(me + s, grid_cols), PICK + s * occ + o)
        used = [jnp.where(pick > 0, 1, 0) for pick in picks]
        near = jnp.where(even, jnp.maximum(used[1], used[2]), jnp.maximum(used[2], used[3]))
        one = jnp.where(even, used[3], used[1])
        near_sum += near
        one_sum += one
        result = own(result, near, me, SEND_NEAR + o)
        result = own(result, one, me, SEND_ONE + o)
        for k in range(2):
            result = own(result, near, lax.rem(near_source + k, grid_cols), RECV_NEAR + k * occ + o)
        result = own(result, one, lax.rem(me + 1 + 2 * core, grid_cols), RECV_ONE + o)
    level = jnp.zeros((1, 1), jnp.int32)
    near_most = jnp.zeros((1, grid_cols), jnp.int32)
    pair_most = jnp.zeros((1, grid_cols), jnp.int32)
    one_most = jnp.zeros((1, grid_cols), jnp.int32)
    for r in range(grid_rows // rows):
        part = slice(r * rows, (r + 1) * rows)
        count = jnp.sum(near_sum[part], axis=0, keepdims=True)
        pair = jnp.where(even[:1], count + jnp.concatenate([count[:, 1:], count[:, :1]], axis=1), 0)
        pair_most = jnp.maximum(pair_most, pair)
        near_most = jnp.maximum(near_most, count)
        one_most = jnp.maximum(one_most, jnp.sum(one_sum[part], axis=0, keepdims=True))
    pair_most = jnp.max(pair_most, axis=1, keepdims=True)
    near_most = jnp.max(near_most, axis=1, keepdims=True)
    one_most = jnp.max(one_most, axis=1, keepdims=True)
    for c2, c1 in ladder(rows * occ)[:-1]:
        over = (pair_most > 2 * c2) | (near_most > c2 + excess(rows * occ, c2)) | (one_most > c1)
        level = jnp.maximum(level, jnp.where(over, 1 + ladder(rows * occ).index((c2, c1)), 0))
    grid_ref[...] = near_sum
    sibling = jnp.where(small_lane == me + 1 - 2 * core, grid_ref[pl.ds(first, rows), :], 0)
    sibling = jnp.sum(jnp.sum(sibling, axis=1, keepdims=True), axis=0, keepdims=True)
    result = jnp.where(out_lane == SIBLING, sibling, result)
    out_ref[...] = jnp.where(out_lane == LEVEL, level, result)


def index_kernel(n_rows, n_cols, mine_ref, out_ref, row_send, row_recv, col_send, col_recv):
    row, col = lax.axis_index("row"), lax.axis_index("col")
    barrier = pltpu.get_barrier_semaphore()
    for d in range(1, n_rows):
        pl.semaphore_signal(barrier, inc=1, device_id={"row": lax.rem(row + d, n_rows)}, device_id_type=MESH)
    for d in range(1, n_cols):
        pl.semaphore_signal(barrier, inc=1, device_id={"col": lax.rem(col + d, n_cols)}, device_id_type=MESH)
    pl.semaphore_wait(barrier, n_rows + n_cols - 2)
    out_ref[col, row] = mine_ref[...]
    copies = [
        pltpu.make_async_remote_copy(
            src_ref=mine_ref, dst_ref=out_ref.at[col, row],
            send_sem=row_send.at[d - 1], recv_sem=row_recv.at[d - 1],
            device_id={"row": lax.rem(row + d, n_rows)}, device_id_type=MESH)
        for d in range(1, n_rows)
    ]
    for copy in copies:
        copy.start()
    for copy in copies:
        copy.wait()
    copies = [
        pltpu.make_async_remote_copy(
            src_ref=out_ref.at[col], dst_ref=out_ref.at[col],
            send_sem=col_send.at[d - 1], recv_sem=col_recv.at[d - 1],
            device_id={"col": lax.rem(col + d, n_cols)}, device_id_type=MESH)
        for d in range(1, n_cols)
    ]
    for copy in copies:
        copy.start()
    for copy in copies:
        copy.wait()


def pack_kernel(occ, plan_ref, a_ref, near_ref, one_ref, stage, in_sems, out_sems):
    rows = plan_ref.shape[0]

    def each(act):
        def row(v, counts):
            near, one = counts
            for o in range(occ):
                take_near = plan_ref[v, SEND_NEAR + o]
                take_one = plan_ref[v, SEND_ONE + o]
                act(v * occ + o, near, one, take_near, take_one)
                near, one = near + take_near, one + take_one
            return near, one

        lax.fori_loop(0, rows, row, (jnp.int32(0), jnp.int32(0)))

    def load(i):
        return pltpu.make_async_copy(a_ref.at[i], stage.at[i], in_sems.at[i])

    def store_near(i, near):
        return pltpu.make_async_copy(stage.at[i], near_ref.at[near], out_sems.at[0, near])

    def store_one(i, one):
        return pltpu.make_async_copy(stage.at[i], one_ref.at[one], out_sems.at[1, one])

    def start_loads(i, near, one, take_near, take_one):
        @pl.when(take_near + take_one > 0)
        def _():
            load(i).start()

    def start_stores(i, near, one, take_near, take_one):
        @pl.when(take_near + take_one > 0)
        def _():
            load(i).wait()

        @pl.when(take_near > 0)
        def _():
            store_near(i, near).start()

        @pl.when(take_one > 0)
        def _():
            store_one(i, one).start()

    def wait_stores(i, near, one, take_near, take_one):
        @pl.when(take_near > 0)
        def _():
            store_near(i, near).wait()

        @pl.when(take_one > 0)
        def _():
            store_one(i, one).wait()

    each(start_loads)
    each(start_stores)
    each(wait_stores)


def parts_of(c2, spare):
    parts = []
    for low, high in ((0, c2 - spare), (c2 - spare, c2)):
        parts += [(start, min(CHUNK, high - start)) for start in range(low, high, CHUNK)]
    return parts


def exchange_kernel(c2, c1, spare, n_rows, n, plan_ref, packed_near, packed_one, b_ref,
                    near_ref, one_ref, halo_ref, held, tail, extra, tail_sem, extra_send, extra_recv,
                    near_send, near_recv, held_send, held_recv, fwd_send, fwd_recv,
                    one_send, one_recv, halo_send, halo_recv):
    me, my_row = lax.axis_index("col"), lax.axis_index("row")
    core, side = lax.rem(me, 2), lax.rem(me // 2, 2)
    relays = core + side == 1

    def at(distance):
        return lax.rem(me + n + distance, n)

    row_to, row_from = lax.rem(my_row + n_rows - 1, n_rows), lax.rem(my_row + 1, n_rows)
    one_to, one_from = at(2 * core - 3), at(1 + 2 * core)
    sibling = me + 1 - 2 * core
    held_to = at(2 - 6 * core)
    passed_to = at(6 * core - 4)
    barrier = pltpu.get_barrier_semaphore()
    for other in (one_to, one_from, at(2 - 4 * side)):
        pl.semaphore_signal(barrier, inc=1, device_id={"col": other}, device_id_type=MESH)
    for other in (row_to, row_from):
        pl.semaphore_signal(barrier, inc=1, device_id={"row": other}, device_id_type=MESH)

    @pl.when(relays)
    def _():
        for other in (at(4), at(-4)):
            pl.semaphore_signal(barrier, inc=1, device_id={"col": other}, device_id_type=MESH)
        pl.semaphore_wait(barrier, 7)

    @pl.when(jnp.logical_not(relays))
    def _():
        pl.semaphore_wait(barrier, 5)

    halo = pltpu.make_async_remote_copy(
        src_ref=b_ref.at[pl.ds(0, halo_ref.shape[0])], dst_ref=halo_ref,
        send_sem=halo_send, recv_sem=halo_recv,
        device_id={"row": row_to}, device_id_type=MESH)
    one = pltpu.make_async_remote_copy(
        src_ref=packed_one.at[pl.ds(0, c1)], dst_ref=one_ref,
        send_sem=one_send, recv_sem=one_recv,
        device_id={"col": one_to}, device_id_type=MESH)
    if spare:
        own_tail = pltpu.make_async_copy(packed_near.at[pl.ds(c2 - spare, spare)], tail, tail_sem)
        over = pltpu.make_async_remote_copy(
            src_ref=packed_near.at[pl.ds(c2, spare)], dst_ref=extra,
            send_sem=extra_send, recv_sem=extra_recv,
            device_id={"col": sibling}, device_id_type=MESH)
        over.start()
        own_tail.start()
    parts = parts_of(c2, spare)
    chunks = len(parts)
    straight, first, second, forward = [], [], [], []
    for c, (start, size) in enumerate(parts):
        part = pl.ds(start, size)
        if start >= c2 - spare:
            source = tail.at[pl.ds(start - (c2 - spare), size)]
        else:
            source = packed_near.at[part]
        straight.append(pltpu.make_async_remote_copy(
            src_ref=source, dst_ref=near_ref.at[core, part],
            send_sem=near_send.at[c], recv_sem=near_recv.at[c],
            device_id={"col": at(-2)}, device_id_type=MESH))
        first.append(pltpu.make_async_remote_copy(
            src_ref=source, dst_ref=held.at[part],
            send_sem=near_send.at[c], recv_sem=held_recv.at[c],
            device_id={"col": held_to}, device_id_type=MESH))
        second.append(pltpu.make_async_remote_copy(
            src_ref=held.at[part], dst_ref=near_ref.at[core, part],
            send_sem=held_send.at[c], recv_sem=near_recv.at[c],
            device_id={"col": passed_to}, device_id_type=MESH))
        forward.append(pltpu.make_async_remote_copy(
            src_ref=near_ref.at[core, part], dst_ref=near_ref.at[core, part],
            send_sem=fwd_send.at[c], recv_sem=fwd_recv.at[c],
            device_id={"col": sibling}, device_id_type=MESH))

    def send(some):
        @pl.when(side == 1)
        def _():
            for c in some:
                straight[c].start()

        @pl.when(side == 0)
        def _():
            for c in some:
                first[c].start()

    whole = [c for c in range(chunks) if parts[c][0] < c2 - spare]
    send(whole)
    halo.start()
    if spare:
        own_tail.wait()
        over.wait_recv()
        count = plan_ref[0:1, SIBLING:SIBLING + 1] - c2
        for t in range(spare):
            tail[spare - 1 - t] = jnp.where(count > t, extra[t], tail[spare - 1 - t])
        send(range(len(whole), chunks))
    for c in range(chunks + LAG):
        if c == LAG + chunks // 3:
            one.start()
        if c < chunks:
            @pl.when(relays)
            def _(c=c):
                first[c].wait_recv()
                second[c].start()

        if c >= LAG:
            straight[c - LAG].wait_recv()
            forward[c - LAG].start()
    one.wait()
    halo.wait()
    if spare:
        over.wait_send()
    for c in range(chunks):
        straight[c].wait_send()
        forward[c].wait()

    @pl.when(relays)
    def _():
        for copy in second:
            copy.wait_send()


def product_kernel(occ, c2, plan_ref, a_ref, b_ref, halo_ref, near_ref, one_ref, out_ref,
                   a_items, b_items, v_items, a_buf, b_buf, total, a_sem, b_sem, out_sem):
    rows = plan_ref.shape[0]
    odd = lax.rem(lax.axis_index("col"), 2)
    own = rows * occ
    near_end = own + 2 * c2

    def row(v, carry):
        count, near0, near1, one = carry
        for o in range(occ):
            at_near0 = own + jnp.where(near0 < c2, near0, 3 * c2 - 1 - near0)
            at_near1 = own + jnp.where(near1 < c2, c2 + near1, 2 * c2 - 1 - near1)
            at_one = near_end + one
            sources = (v * occ + o,
                       jnp.where(odd == 1, at_near0, at_one),
                       jnp.where(odd == 1, at_near1, at_near0),
                       jnp.where(odd == 1, at_one, at_near1))
            for s in range(SECTIONS):
                pick = plan_ref[v, PICK + s * occ + o]
                a_items[count] = sources[s]
                b_items[count] = (v + s) * occ + pick - 1
                v_items[count] = v
                count = count + jnp.where(pick > 0, 1, 0)
            near0 = near0 + plan_ref[v, RECV_NEAR + o]
            near1 = near1 + plan_ref[v, RECV_NEAR + occ + o]
            one = one + plan_ref[v, RECV_ONE + o]
        return count, near0, near1, one

    zero = jnp.int32(0)
    count, _, _, _ = lax.fori_loop(0, rows, row, (zero, zero, zero, zero))
    a_items[count] = 0
    b_items[count] = 0
    v_items[count] = rows
    count = (count + 1) // 2 * 2

    def fetch(i):
        slot = lax.rem(i, BUFFERS)
        a_at, b_at = a_items[i], b_items[i]

        @pl.when(a_at < own)
        def _():
            pltpu.make_async_copy(a_ref.at[a_at], a_buf.at[slot], a_sem.at[slot]).start()

        @pl.when((a_at >= own) & (a_at < near_end))
        def _():
            pltpu.make_async_copy(near_ref.at[a_at - own], a_buf.at[slot], a_sem.at[slot]).start()

        @pl.when(a_at >= near_end)
        def _():
            pltpu.make_async_copy(one_ref.at[a_at - near_end], a_buf.at[slot], a_sem.at[slot]).start()

        @pl.when(b_at < own)
        def _():
            pltpu.make_async_copy(b_ref.at[b_at], b_buf.at[slot], b_sem.at[slot]).start()

        @pl.when(b_at >= own)
        def _():
            pltpu.make_async_copy(halo_ref.at[b_at - own], b_buf.at[slot], b_sem.at[slot]).start()

    def ahead(i, carry):
        fetch(i)
        return carry

    lax.fori_loop(0, jnp.minimum(count, BUFFERS - 2), ahead, 0)
    total[...] = jnp.zeros_like(total)

    def multiply(slot):
        a, b = a_buf[slot], b_buf[slot]
        a_hi, b_hi = a.astype(jnp.bfloat16), b.astype(jnp.bfloat16)
        a_lo = (a - a_hi.astype(jnp.float32)).astype(jnp.bfloat16)
        b_lo = (b - b_hi.astype(jnp.float32)).astype(jnp.bfloat16)
        dot = functools.partial(jnp.dot, preferred_element_type=jnp.float32)
        return dot(a_hi, b_hi) + (dot(a_hi, b_lo) + dot(a_lo, b_hi))

    def pair(k, carry):
        i = 2 * k

        @pl.when(i + BUFFERS - 2 < count)
        def _():
            fetch(i + BUFFERS - 2)
            fetch(i + BUFFERS - 1)

        slots = lax.rem(i, BUFFERS), lax.rem(i + 1, BUFFERS)
        for slot in slots:
            pltpu.make_async_copy(a_ref.at[0], a_buf.at[slot], a_sem.at[slot]).wait()
            pltpu.make_async_copy(b_ref.at[0], b_buf.at[slot], b_sem.at[slot]).wait()
        left, right = multiply(slots[0]), multiply(slots[1])
        total[v_items[i]] += left
        total[v_items[i + 1]] += right
        return carry

    lax.fori_loop(0, count // 2, pair, 0)
    result = pltpu.make_async_copy(total.at[pl.ds(0, rows)], out_ref, out_sem)
    result.start()
    result.wait()


def local(a_values, a_columns, b_values, b_rows):
    rows, _, _, occ, bs, _ = a_values.shape
    n_rows, n_cols = lax.axis_size("row"), lax.axis_size("col")
    block = (bs, bs)
    a_own = a_values.reshape(rows * occ, *block)
    b_own = b_values.reshape(rows * occ, *block)

    vmem = pl.BlockSpec(memory_space=pltpu.VMEM)
    smem = pl.BlockSpec(memory_space=pltpu.SMEM)
    any_ = pl.BlockSpec(memory_space=pl.ANY)
    dma = pltpu.SemaphoreType.DMA
    f32 = jnp.float32
    slots = rows * occ
    steps = ladder(slots)

    with jax.named_scope("indices"):
        both = jnp.concatenate([a_columns[:, 0, 0], b_rows[:, 0, 0]], axis=1)
        both = jnp.pad(both, ((0, 0), (0, LANES - 2 * occ)))
        gathered = pl.pallas_call(
            functools.partial(index_kernel, n_rows, n_cols),
            out_shape=jax.ShapeDtypeStruct((n_cols, n_rows, rows, LANES), jnp.int32),
            in_specs=[vmem],
            out_specs=vmem,
            scratch_shapes=[dma((max(n_rows - 1, 1),))] * 2 + [dma((n_cols - 1,))] * 2,
            compiler_params=pltpu.CompilerParams(collective_id=len(steps), has_side_effects=True),
            name="indices",
        )(both)
        gathered = gathered[..., :2 * occ].transpose(3, 1, 2, 0)
        gathered = gathered.reshape(2 * occ, n_rows * rows, n_cols)
        a_grid, b_grid = gathered[:occ], gathered[occ:]
        b_grid = jnp.concatenate([b_grid, b_grid[:, :HALO]], axis=1)
        b_grid = jnp.concatenate([b_grid[:, :, -HALO:], b_grid], axis=2)

    plan = pl.pallas_call(
        functools.partial(plan_kernel, rows),
        out_shape=jax.ShapeDtypeStruct((rows, LANES), jnp.int32),
        in_specs=[vmem, vmem],
        out_specs=vmem,
        scratch_shapes=[pltpu.VMEM((n_rows * rows, n_cols), jnp.int32)],
        name="plan",
    )(a_grid, b_grid)

    packed_near, packed_one = pl.pallas_call(
        functools.partial(pack_kernel, occ),
        out_shape=[jax.ShapeDtypeStruct((slots, *block), f32)] * 2,
        in_specs=[smem, any_],
        out_specs=[any_, any_],
        scratch_shapes=[pltpu.VMEM((slots, *block), f32), dma((slots,)), dma((2, slots))],
        compiler_params=pltpu.CompilerParams(vmem_limit_bytes=56 << 20),
        name="pack",
    )(plan, a_own)

    def branch(number, c2, c1):
        def run(plan, a_own, b_own, packed_near, packed_one):
            spare = excess(slots, c2)
            chunks = len(parts_of(c2, spare))
            near, one, halo = pl.pallas_call(
                functools.partial(exchange_kernel, c2, c1, spare, n_rows, n_cols),
                out_shape=[jax.ShapeDtypeStruct((2, c2, *block), f32),
                           jax.ShapeDtypeStruct((c1, *block), f32),
                           jax.ShapeDtypeStruct((HALO * occ, *block), f32)],
                in_specs=[vmem] + [any_] * 3,
                out_specs=[any_] * 3,
                scratch_shapes=[pltpu.VMEM((c2, *block), f32)] + [pltpu.VMEM((max(spare, 1), *block), f32)] * 2
                + [dma] * 3 + [dma((chunks,))] * 6 + [dma] * 4,
                compiler_params=pltpu.CompilerParams(
                    collective_id=number, has_side_effects=True, vmem_limit_bytes=56 << 20),
                name="exchange",
            )(plan, packed_near, packed_one, b_own)
            items = pltpu.SMEM((rows * occ * SECTIONS + 8,), jnp.int32)
            return pl.pallas_call(
                functools.partial(product_kernel, occ, c2),
                out_shape=jax.ShapeDtypeStruct((rows, *block), f32),
                in_specs=[smem] + [any_] * 5,
                out_specs=any_,
                scratch_shapes=[items, items, items,
                                pltpu.VMEM((BUFFERS, *block), f32), pltpu.VMEM((BUFFERS, *block), f32),
                                pltpu.VMEM((rows + 1, *block), f32),
                                dma((BUFFERS,)), dma((BUFFERS,)), dma],
                compiler_params=pltpu.CompilerParams(vmem_limit_bytes=62 << 20),
                name="product",
            )(plan, a_own, b_own, halo, near.reshape(2 * c2, *block), one)

        return run

    branches = [branch(number, c2, c1) for number, (c2, c1) in enumerate(steps)]
    out = lax.switch(plan[0, LEVEL], branches, plan, a_own, b_own, packed_near, packed_one)
    return out.reshape(rows, 1, 1, 1, *block)


def solution(mesh):
    return jax.shard_map(
        local,
        mesh=mesh,
        in_specs=(
            P("row", "col", None, None, None, None),
            P("row", "col", None, None),
            P("row", "col", None, None, None, None),
            P("row", "col", None, None),
        ),
        out_specs=P("row", "col", None, None, None, None),
        check_vma=False,
    )
```
